32 devices in a mesh: gx: 4 (over y, core), gy: 8 (over z, x).
Axes of the slice: x: 2, y: 2, z: 4, core: 2. Of those that a mesh axis runs over, the one named last changes fastest.
Arguments:
- right_side: float32 [128, 256, 256], P('gx', 'gy'), may hold values from -32 to 32
- phase: int32 [128, 256, 256], P('gx', 'gy'), may hold values from 1 to 3
- table: float32 [4], replicated, may hold values from 0.3 to 3
Outputs:
- solution_field: float32 [128, 256, 256], P('gx', 'gy')
- residual: float32 [128, 256, 256], P('gx', 'gy')
- pre_residual: float32 [128, 256, 256], P('gx', 'gy')
- residual_image: float32 [128, 256, 256], P('gx', 'gy')
The draws below stay inside these ranges and needn't reach their ends.
Inputs may be any that keep to these rules, and one draw needn't show every extreme that they name: `phase`: labels 1 slag, 2 steel, 3 argon plume; label 0 stands for the lining outside the grid.
All inputs are finite; a program needn't handle non-finite values.
Results may differ from the reference program's by a relative error of at most 0.0003.
Values sent between devices are 32-bit elements; how exact they have to be, the bound alone decides.
A program may use at most 64 MiB of HBM per device.

```python
import math
import jax
import jax.numpy as jnp

ITERS = 2
NCOND = 4
NX = 128
NY = 256
NZ = 256


def draw_right_side(key, part):
    first_key = jax.random.fold_in(key, 11)
    along_x = (jnp.arange(NX, dtype=jnp.float32) + 0.5) / NX
    along_y = (jnp.arange(NY, dtype=jnp.float32) + 0.5) / NY
    ramp = jnp.exp(1.1 * (along_x[:, None, None] + along_y[None, :, None]) - 1.1)
    base = jnp.clip(jax.random.normal(first_key, (NX, NY, NZ), jnp.float32), -6.0, 6.0)
    return (2.0 * ramp * base).astype(jnp.float32)


def set_ends(drawn, key, least, high):
    longest = drawn.shape.index(max(drawn.shape))
    spots = []
    for shift in (0, 1):
        where = [jax.random.randint(jax.random.fold_in(key, axis), (), 0, length) for axis, length in enumerate(drawn.shape)]
        where[longest] = (where[longest] + shift) % drawn.shape[longest]
        spots.append(tuple(where))
    return drawn.at[spots[0]].set(least).at[spots[1]].set(high)


def setup_inputs(seed: int = 0) -> dict:
    key_list = jax.random.split(jax.random.key(seed), 4)
    return {
        "right_side": draw_right_side(jax.random.fold_in(key_list[3], 71), 0),
        "phase": set_ends(jax.random.randint(key_list[1], (NX, NY, NZ), 1, 4), jax.random.fold_in(key_list[1], 1), 1, 3).astype(jnp.int32),
        "table": jnp.clip(jnp.exp(jax.random.uniform(key_list[2], (NCOND,), jnp.float32, math.log(0.3), math.log(3.0))), 0.3, 3.0),
    }


centre_value = 1.1
half_width = 0.9
ratio_sigma = centre_value / half_width
rho_first = 1.0 / ratio_sigma
rho_second = 1.0 / (2.0 * ratio_sigma - rho_first)
rho_third = 1.0 / (2.0 * ratio_sigma - rho_second)
start_scale = 1.0 / centre_value
keep_first = rho_second * rho_first
push_first = 2.0 * rho_second / half_width
keep_second = rho_third * rho_second
push_second = 2.0 * rho_third / half_width


def harmonic(left, right):
    return 2.0 * left * right / (left + right)


def coupling_set(sigma_padded):
    centre = sigma_padded[1:-1, 1:-1, 1:-1]
    to_west = harmonic(centre, sigma_padded[:-2, 1:-1, 1:-1])
    to_east = harmonic(centre, sigma_padded[2:, 1:-1, 1:-1])
    to_south = harmonic(centre, sigma_padded[1:-1, :-2, 1:-1])
    to_north = harmonic(centre, sigma_padded[1:-1, 2:, 1:-1])
    to_down = harmonic(centre, sigma_padded[1:-1, 1:-1, :-2])
    to_up = harmonic(centre, sigma_padded[1:-1, 1:-1, 2:])
    diagonal = to_west + to_east + to_south + to_north + to_down + to_up
    return (to_west, to_east, to_south, to_north, to_down, to_up, diagonal)


def padded_sigma(phase, table):
    return table[jnp.pad(phase, 1)]


def operate(field, phase, table):
    to_west, to_east, to_south, to_north, to_down, to_up, diagonal = coupling_set(padded_sigma(phase, table))
    padded = jnp.pad(field, 1)
    beside = (to_west * padded[:-2, 1:-1, 1:-1] + to_east * padded[2:, 1:-1, 1:-1]
              + to_south * padded[1:-1, :-2, 1:-1] + to_north * padded[1:-1, 2:, 1:-1]
              + to_down * padded[1:-1, 1:-1, :-2] + to_up * padded[1:-1, 1:-1, 2:])
    return diagonal * field - beside


def precondition(vector, phase, table):
    diagonal = coupling_set(padded_sigma(phase, table))[6]
    first = start_scale * (vector / diagonal)
    change = keep_first * first + push_first * ((vector - operate(first, phase, table)) / diagonal)
    second = first + change
    change = keep_second * change + push_second * ((vector - operate(second, phase, table)) / diagonal)
    return second + change


def reference(right_side, phase, table):
    solution_field = jnp.zeros_like(right_side)
    residual = right_side
    pre_residual = precondition(residual, phase, table)
    residual_image = operate(pre_residual, phase, table)
    image_dir = jnp.zeros_like(right_side)
    pre_dir = jnp.zeros_like(right_side)
    resid_dir = jnp.zeros_like(right_side)
    direction = jnp.zeros_like(right_side)
    energy_prev = jnp.float32(1.0)
    step_prev = jnp.float32(1.0)
    for iteration in range(ITERS):
        energy_now = jnp.sum(residual * pre_residual)
        curvature = jnp.sum(residual_image * pre_residual)
        pre_image = precondition(residual_image, phase, table)
        double_image = operate(pre_image, phase, table)
        if iteration == 0:
            step_size = energy_now / curvature
            image_dir = double_image
            pre_dir = pre_image
            resid_dir = residual_image
            direction = pre_residual
        else:
            momentum = energy_now / energy_prev
            step_size = energy_now / (curvature - momentum * energy_now / step_prev)
            image_dir = double_image + momentum * image_dir
            pre_dir = pre_image + momentum * pre_dir
            resid_dir = residual_image + momentum * resid_dir
            direction = pre_residual + momentum * direction
        solution_field = solution_field + step_size * direction
        residual = residual - step_size * resid_dir
        pre_residual = pre_residual - step_size * pre_dir
        residual_image = residual_image - step_size * image_dir
        energy_prev = energy_now
        step_prev = step_size
    return (solution_field, residual, pre_residual, residual_image)
```

```python
import functools

import jax
import jax.numpy as jnp
from jax import lax
from jax.experimental import pallas as pl
from jax.experimental.pallas import tpu as pltpu
from jax.sharding import PartitionSpec as P

MESH = pl.DeviceIdType.MESH

centre_value = 1.1
half_width = 0.9
ratio_sigma = centre_value / half_width
rho_first = 1.0 / ratio_sigma
rho_second = 1.0 / (2.0 * ratio_sigma - rho_first)
rho_third = 1.0 / (2.0 * ratio_sigma - rho_second)
start_scale = 1.0 / centre_value
keep_first = rho_second * rho_first
push_first = 2.0 * rho_second / half_width
keep_second = rho_third * rho_second
push_second = 2.0 * rho_third / half_width

own_first = start_scale * (1.0 + keep_first) + push_first * (1.0 - start_scale)
near_first = push_first * start_scale
own_second = 1.0 + keep_second - push_second
base_second = push_second - keep_second * start_scale

EXCHANGES = 10


def loop(low, high, body, carry=None):
    count = high - low
    unroll = next(u for u in (4, 5, 3, 2, 1) if count % u == 0)

    def step(k, value):
        for j in range(unroll):
            value = body(low + k * unroll + j, value)
        return value

    return lax.fori_loop(0, count // unroll, step, carry)


def fold(block):
    rows, lanes = block.shape
    tile = block[0:8]
    for k in range(1, rows // 8):
        tile = tile + block[8 * k : 8 * k + 8]
    out = tile[:, 0:128]
    for k in range(1, lanes // 128):
        out = out + tile[:, 128 * k : 128 * k + 128]
    return out


def total(tile):
    return jnp.sum(jnp.sum(tile, axis=0, keepdims=True), axis=1, keepdims=True)


def kernel(
    ngx, ngy,
    right_ref, phase_ref, table_ref,
    x_out, r_out, u_out, w_out,
    rho, cx, cs, cd, diag, inv,
    ys, firsts, seconds, images,
    w_next, r_next, u_next,
    pack_s, pack_n, inv_s, inv_n, side_s, side_n,
    face_x, face_y, gain_x, gain_y,
    halo_x, halo_y, red_x, red_y,
    send_sem, recv_sem, rx_send, rx_recv, ry_send, ry_recv,
):
    nx, ny, nz = right_ref.shape
    gx = lax.axis_index("gx")
    gy = lax.axis_index("gy")
    has = (gx > 0, gx < ngx - 1, gy > 0, gy < ngy - 1)

    barrier = pltpu.get_barrier_semaphore()
    for k in range(1, ngx):
        pl.semaphore_signal(barrier, inc=1, device_id={"gx": lax.rem(gx + k, ngx)}, device_id_type=MESH)
    for k in range(1, ngy):
        pl.semaphore_signal(barrier, inc=1, device_id={"gy": lax.rem(gy + k, ngy)}, device_id_type=MESH)

    def halo(e, side):
        return halo_x.at[e, side] if side < 2 else halo_y.at[e, side - 2]

    def copy_of(e, side, src):
        axis, position = ("gx", gx) if side < 2 else ("gy", gy)
        step = -1 if side % 2 == 0 else 1
        return pltpu.make_async_remote_copy(
            src_ref=src,
            dst_ref=halo(e, side ^ 1),
            send_sem=send_sem.at[e, side],
            recv_sem=recv_sem.at[e, side ^ 1],
            device_id={axis: position + step},
            device_id_type=MESH,
        )

    sent = []

    def send(e, sources):
        for side in range(4):
            pl.when(has[side])(functools.partial(lambda c: c.start(), copy_of(e, side, sources[side])))
        sent.append((e, sources))

    def arrive(e):
        for side in range(4):
            dummy = pltpu.make_async_remote_copy(
                src_ref=halo(e, side),
                dst_ref=halo(e, side),
                send_sem=send_sem.at[e, side],
                recv_sem=recv_sem.at[e, side],
                device_id={"gx": gx, "gy": gy},
                device_id_type=MESH,
            )
            pl.when(has[side])(functools.partial(lambda c: c.wait_recv(), dummy))

    t1, t2, t3 = (jnp.full((1, 1), table_ref[k], jnp.float32) for k in (1, 2, 3))
    q0 = 1.0 / jnp.full((1, 1), table_ref[0], jnp.float32)
    q1, q2, q3 = 1.0 / t1, 1.0 / t2, 1.0 / t3

    for side in range(4):
        def outside(side=side):
            for e in range(EXCHANGES):
                target = halo(e, side)
                fill = jnp.zeros(target.shape, jnp.float32)
                target[...] = fill + q0 if e == 0 else fill

        pl.when(jnp.logical_not(has[side]))(outside)

    def lookup_plane(i, _):
        labels = phase_ref[i]
        value = jnp.where(labels == 1, q1, jnp.where(labels == 2, q2, jnp.where(labels == 3, q3, q0)))
        rho[i] = value
        pack_s[0, pl.ds(i, 1), :] = value[0:1]
        pack_n[0, pl.ds(i, 1), :] = value[ny - 1 : ny]
        right = right_ref[i]
        side_s[4, pl.ds(i, 1), :] = right[0:1]
        side_n[4, pl.ds(i, 1), :] = right[ny - 1 : ny]

    loop(0, nx, lookup_plane)
    pl.semaphore_wait(barrier, ngx - 1 + ngy - 1)
    send(0, (rho.at[0], rho.at[nx - 1], pack_s.at[0], pack_n.at[0]))

    row = lax.broadcasted_iota(jnp.int32, (ny, nz), 0)
    lane = lax.broadcasted_iota(jnp.int32, (ny, nz), 1)
    zero = jnp.zeros((ny, nz), jnp.float32)
    cx[0] = zero
    cx[nx] = zero
    for c in range(3):
        for buffer in (ys, firsts, seconds):
            buffer[c, 0] = zero
            buffer[c, nx + 1] = zero

    def couple_x(i, _):
        cx[i] = 2.0 / (rho[i - 1] + rho[i])

    loop(1, nx, couple_x)

    def couple_rest(i, _):
        here = rho[i]
        south = jnp.where(row == 0, 0.0, 2.0 / (here + pltpu.roll(here, 1, 0)))
        beside = jnp.where(lane == 0, q0, pltpu.roll(here, 1, 1))
        down = 2.0 / (here + beside)
        last = 2.0 / (here[:, nz - 128 :] + q0)
        last = jnp.concatenate([jnp.zeros((ny, nz - 128), jnp.float32), last], axis=1)
        inner = jnp.where(lane == 0, 0.0, down)
        cs[i] = south
        cd[i] = inner
        up = jnp.where(lane == nz - 1, last, pltpu.roll(inner, nz - 1, 1))
        d = cx[i] + cx[i + 1] + south + pltpu.roll(south, ny - 1, 0) + down + up
        diag[i] = d
        side_s[3, pl.ds(i, 1), :] = d[0:1]
        side_n[3, pl.ds(i, 1), :] = d[ny - 1 : ny]

    loop(0, nx, couple_rest)

    def scatter(ref, first, row_s, row_n):
        def one(i, _):
            ref[first + i, 0:1, :] = row_s[pl.ds(i, 1), :]
            ref[first + i, ny - 1 : ny, :] = row_n[pl.ds(i, 1), :]

        loop(1, nx - 1, one)

    def correct(ref, first, row_s, row_n, add_x, add_y):
        edge = (first, first + nx - 1)
        for side in range(2):
            ref[edge[side]] = ref[edge[side]] + add_x(side)
        for side, i in ((0, 0), (1, nx - 1)):
            row_s[i : i + 1, :] = ref[edge[side], 0:1, :]
            row_n[i : i + 1, :] = ref[edge[side], ny - 1 : ny, :]
        row_s[...] = row_s[...] + add_y(0)
        row_n[...] = row_n[...] + add_y(1)
        for side, i in ((0, 0), (1, nx - 1)):
            ref[edge[side], 0:1, :] = row_s[i : i + 1, :]
            ref[edge[side], ny - 1 : ny, :] = row_n[i : i + 1, :]

    arrive(0)
    for side, plane in ((0, 0), (1, nx - 1)):
        face_x[side] = 2.0 / (rho[plane] + halo_x[0, side])
    face_y[0] = 2.0 / (pack_s[0] + halo_y[0, 0])
    face_y[1] = 2.0 / (pack_n[0] + halo_y[0, 1])
    ds_, dn_ = side_s.at[3], side_n.at[3]
    correct(diag, 0, ds_, dn_, lambda s: face_x[s], lambda s: face_y[s])
    inv_s[...] = 1.0 / ds_[...]
    inv_n[...] = 1.0 / dn_[...]
    for side, plane in ((0, 0), (1, nx - 1)):
        inv[plane] = 1.0 / diag[plane]
        gain_x[side] = face_x[side] * inv[plane]
    gain_y[0] = face_y[0] * inv_s[...]
    gain_y[1] = face_y[1] * inv_n[...]

    def near(f, i):
        here = f[i + 1]
        south = cs[i]
        down = cd[i]
        return (
            (cx[i] * f[i] + cx[i + 1] * f[i + 2])
            + (south * pltpu.roll(here, 1, 0) + pltpu.roll(south * here, ny - 1, 0))
            + (down * pltpu.roll(here, 1, 1) + pltpu.roll(down * here, nz - 1, 1))
        )

    def send_y(e, y, plane_value, value_s, value_n):
        for plane in (0, nx - 1):
            y[plane + 1] = plane_value(plane) * inv[plane]
        pack_s[e] = value_s * inv_s[...]
        pack_n[e] = value_n * inv_n[...]
        send(e, (y.at[1], y.at[nx], pack_s.at[e], pack_n.at[e]))

    def gained(scale, e):
        return (
            lambda s: (scale * gain_x[s]) * halo_x[e, s],
            lambda s: (scale * gain_y[s]) * halo_y[e, s],
        )

    def composite(c, e, between):
        y, first, second, image = ys.at[c], firsts.at[c], seconds.at[c], images.at[c]

        def step_first(i, _):
            value = own_first * y[i + 1] + near_first * (inv[i] * near(y, i))
            first[i + 1] = value
            pack_s[e + 1, pl.ds(i, 1), :] = value[0:1]
            pack_n[e + 1, pl.ds(i, 1), :] = value[ny - 1 : ny]

        loop(0, nx, step_first)
        arrive(e)
        row_s, row_n = pack_s.at[e + 1], pack_n.at[e + 1]
        correct(first, 1, row_s, row_n, *gained(near_first, e))
        send(e + 1, (first.at[1], first.at[nx], row_s, row_n))
        scatter(first, 1, row_s, row_n)
        between(0)

        def step_second(i, _):
            value = own_second * first[i + 1] + base_second * y[i + 1] + push_second * (inv[i] * near(first, i))
            second[i + 1] = value
            pack_s[e + 2, pl.ds(i, 1), :] = value[0:1]
            pack_n[e + 2, pl.ds(i, 1), :] = value[ny - 1 : ny]

        loop(0, nx, step_second)
        arrive(e + 1)
        row_s2, row_n2 = pack_s.at[e + 2], pack_n.at[e + 2]
        correct(second, 1, row_s2, row_n2, *gained(push_second, e + 1))
        send(e + 2, (second.at[1], second.at[nx], row_s2, row_n2))
        scatter(second, 1, row_s2, row_n2)
        between(1)

        def step_image(i, _):
            value = diag[i] * second[i + 1] - near(second, i)
            image[i] = value
            side_s[c, pl.ds(i, 1), :] = value[0:1]
            side_n[c, pl.ds(i, 1), :] = value[ny - 1 : ny]

        loop(0, nx, step_image)
        arrive(e + 2)
        correct(
            image, 0, side_s.at[c], side_n.at[c],
            lambda s: -(face_x[s] * halo_x[e + 2, s]),
            lambda s: -(face_y[s] * halo_y[e + 2, s]),
        )

    def reduce_start(buffer, axis, position, count, send_sems, recv_sems):
        for k in range(1, count):
            reduce_copy(buffer, axis, position, count, k, send_sems, recv_sems).start()

    def reduce_copy(buffer, axis, position, count, k, send_sems, recv_sems):
        return pltpu.make_async_remote_copy(
            src_ref=buffer.at[0],
            dst_ref=buffer.at[k],
            send_sem=send_sems.at[k],
            recv_sem=recv_sems.at[k],
            device_id={axis: lax.rem(position + k, count)},
            device_id_type=MESH,
        )

    def reduce_end(buffer, axis, position, count, send_sems, recv_sems):
        value = buffer[0]
        for k in range(1, count):
            reduce_copy(buffer, axis, position, count, k, send_sems, recv_sems).wait()
            value = value + buffer[k]
        return value

    def over_x(t):
        return red_x.at[t], "gx", gx, ngx, rx_send.at[t], rx_recv.at[t]

    def over_y(t):
        return red_y.at[t], "gy", gy, ngy, ry_send.at[t], ry_recv.at[t]

    def put_sums(t, sums):
        red_x[t, 0, 0:8, :] = sums[0]
        red_x[t, 0, 8:16, :] = sums[1]
        reduce_start(*over_x(t))

    def relay(t):
        red_y[t, 0] = reduce_end(*over_x(t))
        reduce_start(*over_y(t))

    def take_sums(t):
        both = reduce_end(*over_y(t))
        return total(both[0:8]), total(both[8:16])

    send_y(1, ys.at[0], lambda p: right_ref[p], side_s[4], side_n[4])
    scatter(diag, 0, ds_, dn_)

    def start_plane(i, _):
        value = 1.0 / diag[i]
        inv[i] = value
        ys[0, i + 1] = right_ref[i] * value

    loop(1, nx - 1, start_plane)
    composite(0, 1, lambda k: None)

    w0, u0 = images.at[0], seconds.at[0]
    send_y(4, ys.at[1], lambda p: w0[p], side_s[0], side_n[0])
    scatter(w0, 0, side_s.at[0], side_n.at[0])
    tile = jnp.zeros((8, 128), jnp.float32)

    def second_plane(i, sums):
        w = w0[i]
        u = u0[i + 1]
        ys[1, i + 1] = w * inv[i]
        return sums[0] + fold(right_ref[i] * u), sums[1] + fold(w * u)

    sums = (tile, tile)
    for plane in (0, nx - 1):
        u = u0[plane + 1]
        sums = (sums[0] + fold(right_ref[plane] * u), sums[1] + fold(w0[plane] * u))
    put_sums(0, loop(1, nx - 1, second_plane, sums))
    composite(1, 4, lambda k: relay(0) if k == 0 else None)
    g0, h0 = take_sums(0)
    a0 = g0 / h0

    m0, n0 = seconds.at[1], images.at[1]
    for plane in (0, nx - 1):
        w_next[plane] = w0[plane] - a0 * n0[plane]
    send_y(7, ys.at[2], lambda p: w_next[p], side_s[0] - a0 * side_s[1], side_n[0] - a0 * side_n[1])
    scatter(n0, 0, side_s.at[1], side_n.at[1])

    def advance(i, sums):
        w = w_next[i]
        r = right_ref[i] - a0 * w0[i]
        u = u0[i + 1] - a0 * m0[i + 1]
        r_next[i] = r
        u_next[i] = u
        return sums[0] + fold(r * u), sums[1] + fold(w * u)

    def third_plane(i, sums):
        w = w0[i] - a0 * n0[i]
        w_next[i] = w
        ys[2, i + 1] = w * inv[i]
        return advance(i, sums)

    sums = (tile, tile)
    for plane in (0, nx - 1):
        sums = advance(plane, sums)
    put_sums(1, loop(1, nx - 1, third_plane, sums))
    composite(2, 7, lambda k: relay(1) if k == 0 else None)
    scatter(images.at[2], 0, side_s.at[2], side_n.at[2])
    g1, h1 = take_sums(1)
    b = g1 / g0
    a1 = g1 / (h1 - b * g1 / a0)

    def finish(i, _):
        u = u_next[i]
        x_out[i] = a0 * u0[i + 1] + a1 * (u + b * u0[i + 1])
        r_out[i] = r_next[i] - a1 * (w_next[i] + b * w0[i])
        u_out[i] = u - a1 * (seconds[2, i + 1] + b * m0[i + 1])
        w_out[i] = w_next[i] - a1 * (images[2, i] + b * n0[i])

    loop(0, nx, finish)

    for e, sources in sent:
        for side in range(4):
            pl.when(has[side])(functools.partial(lambda c: c.wait_send(), copy_of(e, side, sources[side])))


def solution(mesh):
    ngx, ngy = mesh.shape["gx"], mesh.shape["gy"]

    def local(right_side, phase, table):
        nx, ny, nz = right_side.shape
        f32 = jnp.float32
        block = pltpu.VMEM((nx, ny, nz), f32)
        three = pltpu.VMEM((3, nx + 2, ny, nz), f32)
        packed = pltpu.VMEM((EXCHANGES, nx, nz), f32)
        packed_one = pltpu.VMEM((nx, nz), f32)
        sides = pltpu.VMEM((5, nx, nz), f32)
        whole = pl.BlockSpec(memory_space=pltpu.VMEM)
        return pl.pallas_call(
            functools.partial(kernel, ngx, ngy),
            out_shape=[jax.ShapeDtypeStruct((nx, ny, nz), f32)] * 4,
            in_specs=[whole, whole, pl.BlockSpec(memory_space=pltpu.SMEM)],
            out_specs=[whole] * 4,
            scratch_shapes=[
                block, pltpu.VMEM((nx + 1, ny, nz), f32), block, block, block, block,
                three, three, three, pltpu.VMEM((3, nx, ny, nz), f32),
                block, block, block,
                packed, packed, packed_one, packed_one, sides, sides,
                pltpu.VMEM((2, ny, nz), f32), pltpu.VMEM((2, nx, nz), f32),
                pltpu.VMEM((2, ny, nz), f32), pltpu.VMEM((2, nx, nz), f32),
                pltpu.VMEM((EXCHANGES, 2, ny, nz), f32), pltpu.VMEM((EXCHANGES, 2, nx, nz), f32),
                pltpu.VMEM((2, ngx, 16, 128), f32), pltpu.VMEM((2, ngy, 16, 128), f32),
                pltpu.SemaphoreType.DMA((EXCHANGES, 4)), pltpu.SemaphoreType.DMA((EXCHANGES, 4)),
                pltpu.SemaphoreType.DMA((2, ngx)), pltpu.SemaphoreType.DMA((2, ngx)),
                pltpu.SemaphoreType.DMA((2, ngy)), pltpu.SemaphoreType.DMA((2, ngy)),
            ],
            compiler_params=pltpu.CompilerParams(
                collective_id=0, has_side_effects=True, vmem_limit_bytes=56 * 1024 * 1024
            ),
        )(right_side, phase, table)

    spec = P("gx", "gy", None)
    return jax.shard_map(
        local, mesh=mesh, in_specs=(spec, spec, P()), out_specs=(spec,) * 4, check_vma=False
    )
```

```python
import functools

import jax
import jax.numpy as jnp
from jax import lax
from jax.experimental import pallas as pl
from jax.experimental.pallas import tpu as pltpu
from jax.sharding import PartitionSpec as P

MESH = pl.DeviceIdType.MESH

centre_value = 1.1
half_width = 0.9
ratio_sigma = centre_value / half_width
rho_first = 1.0 / ratio_sigma
rho_second = 1.0 / (2.0 * ratio_sigma - rho_first)
rho_third = 1.0 / (2.0 * ratio_sigma - rho_second)
start_scale = 1.0 / centre_value
keep_first = rho_second * rho_first
push_first = 2.0 * rho_second / half_width
keep_second = rho_third * rho_second
push_second = 2.0 * rho_third / half_width

own_first = start_scale * (1.0 + keep_first) + push_first * (1.0 - start_scale)
near_first = push_first * start_scale
own_second = 1.0 + keep_second - push_second
base_second = push_second - keep_second * start_scale

EXCHANGES = 10


def loop(low, high, body, carry=None):
    count = high - low
    unroll = next(u for u in (4, 5, 3, 2, 1) if count % u == 0)

    def step(k, value):
        for j in range(unroll):
            value = body(low + k * unroll + j, value)
        return value

    return lax.fori_loop(0, count // unroll, step, carry)


def fold(block):
    rows, lanes = block.shape
    tile = block[0:8]
    for k in range(1, rows // 8):
        tile = tile + block[8 * k : 8 * k + 8]
    out = tile[:, 0:128]
    for k in range(1, lanes // 128):
        out = out + tile[:, 128 * k : 128 * k + 128]
    return out


def total(tile):
    return jnp.sum(jnp.sum(tile, axis=0, keepdims=True), axis=1, keepdims=True)


def kernel(
    ngx, ngy,
    right_ref, phase_ref, table_ref,
    seconds, images, steps,
    rho, cx, cs, cd, diag, inv,
    ys, firsts, w_next,
    pack_s, pack_n, inv_s, inv_n, side_s, side_n,
    face_x, face_y, gain_x, gain_y,
    halo_x, halo_y, red_x, red_y,
    send_sem, recv_sem, rx_send, rx_recv, ry_send, ry_recv,
):
    nx, ny, nz = right_ref.shape
    gx = lax.axis_index("gx")
    gy = lax.axis_index("gy")
    has = (gx > 0, gx < ngx - 1, gy > 0, gy < ngy - 1)

    barrier = pltpu.get_barrier_semaphore()
    for k in range(1, ngx):
        pl.semaphore_signal(barrier, inc=1, device_id={"gx": lax.rem(gx + k, ngx)}, device_id_type=MESH)
    for k in range(1, ngy):
        pl.semaphore_signal(barrier, inc=1, device_id={"gy": lax.rem(gy + k, ngy)}, device_id_type=MESH)

    def halo(e, side):
        return halo_x.at[e, side] if side < 2 else halo_y.at[e, side - 2]

    def copy_of(e, side, src):
        axis, position = ("gx", gx) if side < 2 else ("gy", gy)
        step = -1 if side % 2 == 0 else 1
        return pltpu.make_async_remote_copy(
            src_ref=src,
            dst_ref=halo(e, side ^ 1),
            send_sem=send_sem.at[e, side],
            recv_sem=recv_sem.at[e, side ^ 1],
            device_id={axis: position + step},
            device_id_type=MESH,
        )

    sent = []

    def send(e, side, source):
        pl.when(has[side])(functools.partial(lambda c: c.start(), copy_of(e, side, source)))
        sent.append((e, side, source))

    def arrive(e, sides):
        for side in sides:
            dummy = pltpu.make_async_remote_copy(
                src_ref=halo(e, side),
                dst_ref=halo(e, side),
                send_sem=send_sem.at[e, side],
                recv_sem=recv_sem.at[e, side],
                device_id={"gx": gx, "gy": gy},
                device_id_type=MESH,
            )
            pl.when(has[side])(functools.partial(lambda c: c.wait_recv(), dummy))

    t1, t2, t3 = (jnp.full((1, 1), table_ref[k], jnp.float32) for k in (1, 2, 3))
    q0 = 1.0 / jnp.full((1, 1), table_ref[0], jnp.float32)
    q1, q2, q3 = 1.0 / t1, 1.0 / t2, 1.0 / t3

    for side in range(4):
        def outside(side=side):
            for e in range(EXCHANGES):
                target = halo(e, side)
                fill = jnp.zeros(target.shape, jnp.float32)
                target[...] = fill + q0 if e == 0 else fill

        pl.when(jnp.logical_not(has[side]))(outside)

    def lookup_plane(i, _):
        labels = phase_ref[i]
        value = jnp.where(labels == 1, q1, jnp.where(labels == 2, q2, jnp.where(labels == 3, q3, q0)))
        rho[i] = value
        pack_s[0, pl.ds(i, 1), :] = value[0:1]
        pack_n[0, pl.ds(i, 1), :] = value[ny - 1 : ny]
        right = right_ref[i]
        side_s[4, pl.ds(i, 1), :] = right[0:1]
        side_n[4, pl.ds(i, 1), :] = right[ny - 1 : ny]

    loop(0, nx, lookup_plane)
    pl.semaphore_wait(barrier, ngx - 1 + ngy - 1)
    send(0, 2, pack_s.at[0])
    send(0, 3, pack_n.at[0])
    send(0, 0, rho.at[0])
    send(0, 1, rho.at[nx - 1])

    row = lax.broadcasted_iota(jnp.int32, (ny, nz), 0)
    lane = lax.broadcasted_iota(jnp.int32, (ny, nz), 1)
    zero = jnp.zeros((ny, nz), jnp.float32)
    cx[0] = zero
    cx[nx] = zero
    for c in range(3):
        for buffer in (ys, firsts, seconds):
            buffer[c, 0] = zero
            buffer[c, nx + 1] = zero

    def couple_x(i, _):
        cx[i] = 2.0 / (rho[i - 1] + rho[i])

    loop(1, nx, couple_x)

    def couple_rest(i, _):
        here = rho[i]
        south = jnp.where(row == 0, 0.0, 2.0 / (here + pltpu.roll(here, 1, 0)))
        beside = jnp.where(lane == 0, q0, pltpu.roll(here, 1, 1))
        down = 2.0 / (here + beside)
        last = 2.0 / (here[:, nz - 128 :] + q0)
        last = jnp.concatenate([jnp.zeros((ny, nz - 128), jnp.float32), last], axis=1)
        inner = jnp.where(lane == 0, 0.0, down)
        cs[i] = south
        cd[i] = inner
        up = jnp.where(lane == nz - 1, last, pltpu.roll(inner, nz - 1, 1))
        d = cx[i] + cx[i + 1] + south + pltpu.roll(south, ny - 1, 0) + down + up
        diag[i] = d
        side_s[3, pl.ds(i, 1), :] = d[0:1]
        side_n[3, pl.ds(i, 1), :] = d[ny - 1 : ny]

    loop(0, nx, couple_rest)

    def scatter(ref, first, row_s, row_n):
        def one(i, _):
            ref[first + i, 0:1, :] = row_s[pl.ds(i, 1), :]
            ref[first + i, ny - 1 : ny, :] = row_n[pl.ds(i, 1), :]

        loop(1, nx - 1, one)

    def settle(e, ref, first, row_s, row_n, add_x, add_y, e_out=None):
        edge = (first, first + nx - 1)
        arrive(e, (0, 1))
        for side, i in ((0, 0), (1, nx - 1)):
            plane = ref[edge[side]] + add_x(side)
            ref[edge[side]] = plane
            row_s[i : i + 1, :] = plane[0:1]
            row_n[i : i + 1, :] = plane[ny - 1 : ny]
        for k, rows in ((0, row_s), (1, row_n)):
            arrive(e, (2 + k,))
            rows[...] = rows[...] + add_y(k)
            if e_out is not None:
                send(e_out, 2 + k, rows)
        for side, i in ((0, 0), (1, nx - 1)):
            ref[edge[side], 0:1, :] = row_s[i : i + 1, :]
            ref[edge[side], ny - 1 : ny, :] = row_n[i : i + 1, :]
            if e_out is not None:
                send(e_out, side, ref.at[edge[side]])

    arrive(0, range(4))
    for side, plane in ((0, 0), (1, nx - 1)):
        face_x[side] = 2.0 / (rho[plane] + halo_x[0, side])
    face_y[0] = 2.0 / (pack_s[0] + halo_y[0, 0])
    face_y[1] = 2.0 / (pack_n[0] + halo_y[0, 1])
    ds_, dn_ = side_s.at[3], side_n.at[3]
    for side, plane in ((0, 0), (1, nx - 1)):
        whole = diag[plane] + face_x[side]
        diag[plane] = whole
        ds_[plane : plane + 1, :] = whole[0:1]
        dn_[plane : plane + 1, :] = whole[ny - 1 : ny]
    ds_[...] = ds_[...] + face_y[0]
    dn_[...] = dn_[...] + face_y[1]
    for plane in (0, nx - 1):
        diag[plane, 0:1, :] = ds_[plane : plane + 1, :]
        diag[plane, ny - 1 : ny, :] = dn_[plane : plane + 1, :]
    inv_s[...] = 1.0 / ds_[...]
    inv_n[...] = 1.0 / dn_[...]
    for side, plane in ((0, 0), (1, nx - 1)):
        inv[plane] = 1.0 / diag[plane]
        gain_x[side] = face_x[side] * inv[plane]
    gain_y[0] = face_y[0] * inv_s[...]
    gain_y[1] = face_y[1] * inv_n[...]

    def near(f, i):
        here = f[i + 1]
        south = cs[i]
        down = cd[i]
        return (
            (cx[i] * f[i] + cx[i + 1] * f[i + 2])
            + (south * pltpu.roll(here, 1, 0) + pltpu.roll(south * here, ny - 1, 0))
            + (down * pltpu.roll(here, 1, 1) + pltpu.roll(down * here, nz - 1, 1))
        )

    def send_y(e, y, plane_value, value_s, value_n):
        pack_s[e] = value_s * inv_s[...]
        send(e, 2, pack_s.at[e])
        pack_n[e] = value_n * inv_n[...]
        send(e, 3, pack_n.at[e])
        for side, plane in ((0, 0), (1, nx - 1)):
            y[plane + 1] = plane_value(plane) * inv[plane]
            send(e, side, y.at[plane + 1])

    def gained(scale, e):
        return (
            lambda s: (scale * gain_x[s]) * halo_x[e, s],
            lambda s: (scale * gain_y[s]) * halo_y[e, s],
        )

    def composite(c, e, between):
        y, first, second, image = ys.at[c], firsts.at[c], seconds.at[c], images.at[c]

        def step_first(i, _):
            value = own_first * y[i + 1] + near_first * (inv[i] * near(y, i))
            first[i + 1] = value
            pack_s[e + 1, pl.ds(i, 1), :] = value[0:1]
            pack_n[e + 1, pl.ds(i, 1), :] = value[ny - 1 : ny]

        loop(0, nx, step_first)
        row_s, row_n = pack_s.at[e + 1], pack_n.at[e + 1]
        settle(e, first, 1, row_s, row_n, *gained(near_first, e), e + 1)
        scatter(first, 1, row_s, row_n)
        between(0)

        def step_second(i, _):
            value = own_second * first[i + 1] + base_second * y[i + 1] + push_second * (inv[i] * near(first, i))
            second[i + 1] = value
            pack_s[e + 2, pl.ds(i, 1), :] = value[0:1]
            pack_n[e + 2, pl.ds(i, 1), :] = value[ny - 1 : ny]

        loop(0, nx, step_second)
        row_s2, row_n2 = pack_s.at[e + 2], pack_n.at[e + 2]
        settle(e + 1, second, 1, row_s2, row_n2, *gained(push_second, e + 1), e + 2)
        scatter(second, 1, row_s2, row_n2)
        between(1)

        def step_image(i, _):
            value = diag[i] * second[i + 1] - near(second, i)
            image[i] = value
            side_s[c, pl.ds(i, 1), :] = value[0:1]
            side_n[c, pl.ds(i, 1), :] = value[ny - 1 : ny]

        loop(0, nx, step_image)
        settle(
            e + 2, image, 0, side_s.at[c], side_n.at[c],
            lambda s: -(face_x[s] * halo_x[e + 2, s]),
            lambda s: -(face_y[s] * halo_y[e + 2, s]),
        )

    def reduce_start(buffer, axis, position, count, send_sems, recv_sems):
        for k in range(1, count):
            reduce_copy(buffer, axis, position, count, k, send_sems, recv_sems).start()

    def reduce_copy(buffer, axis, position, count, k, send_sems, recv_sems):
        return pltpu.make_async_remote_copy(
            src_ref=buffer.at[0],
            dst_ref=buffer.at[k],
            send_sem=send_sems.at[k],
            recv_sem=recv_sems.at[k],
            device_id={axis: lax.rem(position + k, count)},
            device_id_type=MESH,
        )

    def reduce_end(buffer, axis, position, count, send_sems, recv_sems):
        value = buffer[0]
        for k in range(1, count):
            reduce_copy(buffer, axis, position, count, k, send_sems, recv_sems).wait()
            value = value + buffer[k]
        return value

    def over_x(t):
        return red_x.at[t], "gx", gx, ngx, rx_send.at[t], rx_recv.at[t]

    def over_y(t):
        return red_y.at[t], "gy", gy, ngy, ry_send.at[t], ry_recv.at[t]

    def put_sums(t, sums):
        red_x[t, 0, 0:8, :] = sums[0]
        red_x[t, 0, 8:16, :] = sums[1]
        reduce_start(*over_x(t))

    def relay(t):
        red_y[t, 0] = reduce_end(*over_x(t))
        reduce_start(*over_y(t))

    def take_sums(t):
        both = reduce_end(*over_y(t))
        return total(both[0:8]), total(both[8:16])

    send_y(1, ys.at[0], lambda p: right_ref[p], side_s[4], side_n[4])
    scatter(diag, 0, ds_, dn_)

    def start_plane(i, _):
        value = 1.0 / diag[i]
        inv[i] = value
        ys[0, i + 1] = right_ref[i] * value

    loop(1, nx - 1, start_plane)
    composite(0, 1, lambda k: None)

    w0, u0 = images.at[0], seconds.at[0]
    send_y(4, ys.at[1], lambda p: w0[p], side_s[0], side_n[0])
    scatter(w0, 0, side_s.at[0], side_n.at[0])
    tile = jnp.zeros((8, 128), jnp.float32)

    def second_plane(i, sums):
        w = w0[i]
        u = u0[i + 1]
        ys[1, i + 1] = w * inv[i]
        return sums[0] + fold(right_ref[i] * u), sums[1] + fold(w * u)

    sums = (tile, tile)
    for plane in (0, nx - 1):
        u = u0[plane + 1]
        sums = (sums[0] + fold(right_ref[plane] * u), sums[1] + fold(w0[plane] * u))
    put_sums(0, loop(1, nx - 1, second_plane, sums))
    composite(1, 4, lambda k: relay(0) if k == 0 else None)
    g0, h0 = take_sums(0)
    a0 = g0 / h0

    m0, n0 = seconds.at[1], images.at[1]
    for plane in (0, nx - 1):
        w_next[plane] = w0[plane] - a0 * n0[plane]
    send_y(7, ys.at[2], lambda p: w_next[p], side_s[0] - a0 * side_s[1], side_n[0] - a0 * side_n[1])
    scatter(n0, 0, side_s.at[1], side_n.at[1])

    def advance(i, sums):
        w = w_next[i]
        r = right_ref[i] - a0 * w0[i]
        u = u0[i + 1] - a0 * m0[i + 1]
        return sums[0] + fold(r * u), sums[1] + fold(w * u)

    def third_plane(i, sums):
        w = w0[i] - a0 * n0[i]
        w_next[i] = w
        ys[2, i + 1] = w * inv[i]
        return advance(i, sums)

    sums = (tile, tile)
    for plane in (0, nx - 1):
        sums = advance(plane, sums)
    put_sums(1, loop(1, nx - 1, third_plane, sums))
    composite(2, 7, lambda k: relay(1) if k == 0 else None)
    scatter(images.at[2], 0, side_s.at[2], side_n.at[2])
    g1, h1 = take_sums(1)
    b = g1 / g0
    a1 = g1 / (h1 - b * g1 / a0)

    for k, value in enumerate((a0, a1, b)):
        steps[k] = jnp.broadcast_to(value, (8, 128))

    for e, side, source in sent:
        pl.when(has[side])(functools.partial(lambda c: c.wait_send(), copy_of(e, side, source)))


def finish(parts, right_ref, seconds, images, steps, x_out, r_out, u_out, w_out, right, held, in_sem, out_sem):
    nx = right.shape[0]
    span = nx // parts
    fetch = [
        pltpu.make_async_copy(right_ref.at[pl.ds(p * span, span)], right.at[pl.ds(p * span, span)], in_sem.at[p])
        for p in range(parts)
    ]
    for copy in fetch:
        copy.start()
    a0, a1, b = (steps[k][0:1, 0:1] for k in range(3))
    stores = []
    for p in range(parts):
        fetch[p].wait()

        def plane(i, _):
            u0, w0, m0, n0 = seconds[0, i + 1], images[0, i], seconds[1, i + 1], images[1, i]
            u1 = u0 - a0 * m0
            w1 = w0 - a0 * n0
            held[0, i] = a0 * u0 + a1 * (u1 + b * u0)
            held[1, i] = (right[i] - a0 * w0) - a1 * (w1 + b * w0)
            held[2, i] = u1 - a1 * (seconds[2, i + 1] + b * m0)
            held[3, i] = w1 - a1 * (images[2, i] + b * n0)

        loop(p * span, (p + 1) * span, plane)
        for k, out in enumerate((x_out, r_out, u_out, w_out)):
            rows = pl.ds(p * span, span)
            copy = pltpu.make_async_copy(held.at[k, rows], out.at[rows], out_sem.at[k, p])
            copy.start()
            stores.append(copy)
    for copy in stores:
        copy.wait()


def solution(mesh):
    ngx, ngy = mesh.shape["gx"], mesh.shape["gy"]

    def local(right_side, phase, table):
        nx, ny, nz = right_side.shape
        f32 = jnp.float32
        block = pltpu.VMEM((nx, ny, nz), f32)
        three = pltpu.VMEM((3, nx + 2, ny, nz), f32)
        packed = pltpu.VMEM((EXCHANGES, nx, nz), f32)
        packed_one = pltpu.VMEM((nx, nz), f32)
        sides = pltpu.VMEM((5, nx, nz), f32)
        whole = pl.BlockSpec(memory_space=pltpu.VMEM)
        seconds, images, steps = pl.pallas_call(
            functools.partial(kernel, ngx, ngy),
            out_shape=[three, pltpu.VMEM((3, nx, ny, nz), f32), pltpu.VMEM((3, 8, 128), f32)],
            in_specs=[whole, whole, pl.BlockSpec(memory_space=pltpu.SMEM)],
            out_specs=[whole] * 3,
            scratch_shapes=[
                block, pltpu.VMEM((nx + 1, ny, nz), f32), block, block, block, block,
                three, three, block,
                packed, packed, packed_one, packed_one, sides, sides,
                pltpu.VMEM((2, ny, nz), f32), pltpu.VMEM((2, nx, nz), f32),
                pltpu.VMEM((2, ny, nz), f32), pltpu.VMEM((2, nx, nz), f32),
                pltpu.VMEM((EXCHANGES, 2, ny, nz), f32), pltpu.VMEM((EXCHANGES, 2, nx, nz), f32),
                pltpu.VMEM((2, ngx, 16, 128), f32), pltpu.VMEM((2, ngy, 16, 128), f32),
                pltpu.SemaphoreType.DMA((EXCHANGES, 4)), pltpu.SemaphoreType.DMA((EXCHANGES, 4)),
                pltpu.SemaphoreType.DMA((2, ngx)), pltpu.SemaphoreType.DMA((2, ngx)),
                pltpu.SemaphoreType.DMA((2, ngy)), pltpu.SemaphoreType.DMA((2, ngy)),
            ],
            compiler_params=pltpu.CompilerParams(
                collective_id=0, has_side_effects=True, vmem_limit_bytes=40 * 1024 * 1024
            ),
        )(right_side, phase, table)
        parts = next(p for p in (8, 4, 2, 1) if nx % p == 0)
        anywhere = pl.BlockSpec(memory_space=pl.ANY)
        return pl.pallas_call(
            functools.partial(finish, parts),
            out_shape=[jax.ShapeDtypeStruct((nx, ny, nz), f32)] * 4,
            in_specs=[anywhere, whole, whole, whole],
            out_specs=[anywhere] * 4,
            scratch_shapes=[
                block, pltpu.VMEM((4, nx, ny, nz), f32),
                pltpu.SemaphoreType.DMA((parts,)), pltpu.SemaphoreType.DMA((4, parts)),
            ],
            compiler_params=pltpu.CompilerParams(vmem_limit_bytes=20 * 1024 * 1024),
        )(right_side, seconds, images, steps)

    spec = P("gx", "gy", None)
    return jax.shard_map(
        local, mesh=mesh, in_specs=(spec, spec, P()), out_specs=(spec,) * 4, check_vma=False
    )
```

```python
import functools

import jax
import jax.numpy as jnp
from jax import lax
from jax.experimental import pallas as pl
from jax.experimental.pallas import tpu as pltpu
from jax.sharding import PartitionSpec as P

MESH = pl.DeviceIdType.MESH

centre_value = 1.1
half_width = 0.9
ratio_sigma = centre_value / half_width
rho_first = 1.0 / ratio_sigma
rho_second = 1.0 / (2.0 * ratio_sigma - rho_first)
rho_third = 1.0 / (2.0 * ratio_sigma - rho_second)
start_scale = 1.0 / centre_value
keep_first = rho_second * rho_first
push_first = 2.0 * rho_second / half_width
keep_second = rho_third * rho_second
push_second = 2.0 * rho_third / half_width

own_first = start_scale * (1.0 + keep_first) + push_first * (1.0 - start_scale)
near_first = push_first * start_scale
own_second = 1.0 + keep_second - push_second
base_second = push_second - keep_second * start_scale

EXCHANGES = 10


def loop(low, high, body, carry=None):
    count = high - low
    unroll = next(u for u in (4, 5, 3, 2, 1) if count % u == 0)

    def step(k, value):
        for j in range(unroll):
            value = body(low + k * unroll + j, value)
        return value

    return lax.fori_loop(0, count // unroll, step, carry)


def fold(block):
    rows, lanes = block.shape
    tile = block[0:8]
    for k in range(1, rows // 8):
        tile = tile + block[8 * k : 8 * k + 8]
    out = tile[:, 0:128]
    for k in range(1, lanes // 128):
        out = out + tile[:, 128 * k : 128 * k + 128]
    return out


def total(tile):
    return jnp.sum(jnp.sum(tile, axis=0, keepdims=True), axis=1, keepdims=True)


def kernel(
    ngx, ngy,
    right_in, phase_in, table_in,
    x_out, r_out, u_out, w_out,
    right_ref, phase_ref, table_ref,
    seconds, images,
    rho, cx, cs, cd, diag, inv,
    ys, firsts, w_next,
    pack_s, pack_n, inv_s, inv_n, side_s, side_n,
    face_x, face_y, gain_x, gain_y,
    halo_x, halo_y, red_x, red_y,
    send_sem, recv_sem, rx_send, rx_recv, ry_send, ry_recv, in_sem,
):
    nx, ny, nz = right_ref.shape
    gx = lax.axis_index("gx")
    gy = lax.axis_index("gy")
    has = (gx > 0, gx < ngx - 1, gy > 0, gy < ngy - 1)

    parts = next(p for p in (4, 2, 1) if nx % p == 0)
    span = nx // parts
    fetch_table = pltpu.make_async_copy(table_in, table_ref, in_sem.at[parts + 1])
    fetch_table.start()
    fetches = []
    for p in range(parts):
        rows = pl.ds(p * span, span)
        fetches.append(pltpu.make_async_copy(phase_in.at[rows], phase_ref.at[rows], in_sem.at[p]))
        fetches[p].start()
    fetch_right = pltpu.make_async_copy(right_in, right_ref, in_sem.at[parts])
    fetch_right.start()

    barrier = pltpu.get_barrier_semaphore()
    for k in range(1, ngx):
        pl.semaphore_signal(barrier, inc=1, device_id={"gx": lax.rem(gx + k, ngx)}, device_id_type=MESH)
    for k in range(1, ngy):
        pl.semaphore_signal(barrier, inc=1, device_id={"gy": lax.rem(gy + k, ngy)}, device_id_type=MESH)

    def halo(e, side):
        return halo_x.at[e, side] if side < 2 else halo_y.at[e, side - 2]

    def copy_of(e, side, src):
        axis, position = ("gx", gx) if side < 2 else ("gy", gy)
        step = -1 if side % 2 == 0 else 1
        return pltpu.make_async_remote_copy(
            src_ref=src,
            dst_ref=halo(e, side ^ 1),
            send_sem=send_sem.at[e, side],
            recv_sem=recv_sem.at[e, side ^ 1],
            device_id={axis: position + step},
            device_id_type=MESH,
        )

    sent = []

    def send(e, side, source):
        pl.when(has[side])(functools.partial(lambda c: c.start(), copy_of(e, side, source)))
        sent.append((e, side, source))

    def arrive(e, sides):
        for side in sides:
            dummy = pltpu.make_async_remote_copy(
                src_ref=halo(e, side),
                dst_ref=halo(e, side),
                send_sem=send_sem.at[e, side],
                recv_sem=recv_sem.at[e, side],
                device_id={"gx": gx, "gy": gy},
                device_id_type=MESH,
            )
            pl.when(has[side])(functools.partial(lambda c: c.wait_recv(), dummy))

    fetch_table.wait()

    t1, t2, t3 = (jnp.full((1, 1), table_ref[k], jnp.float32) for k in (1, 2, 3))
    q0 = 1.0 / jnp.full((1, 1), table_ref[0], jnp.float32)
    q1, q2, q3 = 1.0 / t1, 1.0 / t2, 1.0 / t3

    for side in range(4):
        def outside(side=side):
            for e in range(EXCHANGES):
                target = halo(e, side)
                fill = jnp.zeros(target.shape, jnp.float32)
                target[...] = fill + q0 if e == 0 else fill

        pl.when(jnp.logical_not(has[side]))(outside)

    def lookup_plane(i, _):
        labels = phase_ref[i]
        value = jnp.where(labels == 1, q1, jnp.where(labels == 2, q2, jnp.where(labels == 3, q3, q0)))
        rho[i] = value
        pack_s[0, pl.ds(i, 1), :] = value[0:1]
        pack_n[0, pl.ds(i, 1), :] = value[ny - 1 : ny]

    for p in range(parts):
        fetches[p].wait()
        loop(p * span, (p + 1) * span, lookup_plane)
    pl.semaphore_wait(barrier, ngx - 1 + ngy - 1)
    send(0, 2, pack_s.at[0])
    send(0, 3, pack_n.at[0])
    send(0, 0, rho.at[0])
    send(0, 1, rho.at[nx - 1])

    row = lax.broadcasted_iota(jnp.int32, (ny, nz), 0)
    lane = lax.broadcasted_iota(jnp.int32, (ny, nz), 1)
    zero = jnp.zeros((ny, nz), jnp.float32)
    cx[0] = zero
    cx[nx] = zero
    for c in range(3):
        for buffer in (ys, firsts, seconds):
            buffer[c, 0] = zero
            buffer[c, nx + 1] = zero

    def couple_x(i, _):
        cx[i] = 2.0 / (rho[i - 1] + rho[i])

    loop(1, nx, couple_x)
    fetch_right.wait()

    def right_rows(i, _):
        right = right_ref[i]
        side_s[4, pl.ds(i, 1), :] = right[0:1]
        side_n[4, pl.ds(i, 1), :] = right[ny - 1 : ny]

    loop(0, nx, right_rows)

    def couple_rest(i, _):
        here = rho[i]
        south = jnp.where(row == 0, 0.0, 2.0 / (here + pltpu.roll(here, 1, 0)))
        beside = jnp.where(lane == 0, q0, pltpu.roll(here, 1, 1))
        down = 2.0 / (here + beside)
        last = 2.0 / (here[:, nz - 128 :] + q0)
        last = jnp.concatenate([jnp.zeros((ny, nz - 128), jnp.float32), last], axis=1)
        inner = jnp.where(lane == 0, 0.0, down)
        cs[i] = south
        cd[i] = inner
        up = jnp.where(lane == nz - 1, last, pltpu.roll(inner, nz - 1, 1))
        d = cx[i] + cx[i + 1] + south + pltpu.roll(south, ny - 1, 0) + down + up
        diag[i] = d
        side_s[3, pl.ds(i, 1), :] = d[0:1]
        side_n[3, pl.ds(i, 1), :] = d[ny - 1 : ny]

    loop(0, nx, couple_rest)

    def scatter(ref, first, row_s, row_n):
        def one(i, _):
            ref[first + i, 0:1, :] = row_s[pl.ds(i, 1), :]
            ref[first + i, ny - 1 : ny, :] = row_n[pl.ds(i, 1), :]

        loop(1, nx - 1, one)

    def settle(e, ref, first, row_s, row_n, add_x, add_y, e_out=None):
        edge = (first, first + nx - 1)
        arrive(e, (0, 1))
        for side, i in ((0, 0), (1, nx - 1)):
            plane = ref[edge[side]] + add_x(side)
            ref[edge[side]] = plane
            row_s[i : i + 1, :] = plane[0:1]
            row_n[i : i + 1, :] = plane[ny - 1 : ny]
        for k, rows in ((0, row_s), (1, row_n)):
            arrive(e, (2 + k,))
            rows[...] = rows[...] + add_y(k)
            if e_out is not None:
                send(e_out, 2 + k, rows)
        for side, i in ((0, 0), (1, nx - 1)):
            ref[edge[side], 0:1, :] = row_s[i : i + 1, :]
            ref[edge[side], ny - 1 : ny, :] = row_n[i : i + 1, :]
            if e_out is not None:
                send(e_out, side, ref.at[edge[side]])

    arrive(0, range(4))
    for side, plane in ((0, 0), (1, nx - 1)):
        face_x[side] = 2.0 / (rho[plane] + halo_x[0, side])
    face_y[0] = 2.0 / (pack_s[0] + halo_y[0, 0])
    face_y[1] = 2.0 / (pack_n[0] + halo_y[0, 1])
    ds_, dn_ = side_s.at[3], side_n.at[3]
    for side, plane in ((0, 0), (1, nx - 1)):
        whole = diag[plane] + face_x[side]
        diag[plane] = whole
        ds_[plane : plane + 1, :] = whole[0:1]
        dn_[plane : plane + 1, :] = whole[ny - 1 : ny]
    ds_[...] = ds_[...] + face_y[0]
    dn_[...] = dn_[...] + face_y[1]
    for plane in (0, nx - 1):
        diag[plane, 0:1, :] = ds_[plane : plane + 1, :]
        diag[plane, ny - 1 : ny, :] = dn_[plane : plane + 1, :]
    inv_s[...] = 1.0 / ds_[...]
    inv_n[...] = 1.0 / dn_[...]
    for side, plane in ((0, 0), (1, nx - 1)):
        inv[plane] = 1.0 / diag[plane]
        gain_x[side] = face_x[side] * inv[plane]
    gain_y[0] = face_y[0] * inv_s[...]
    gain_y[1] = face_y[1] * inv_n[...]

    def near(f, i):
        here = f[i + 1]
        south = cs[i]
        down = cd[i]
        return (
            (cx[i] * f[i] + cx[i + 1] * f[i + 2])
            + (south * pltpu.roll(here, 1, 0) + pltpu.roll(south * here, ny - 1, 0))
            + (down * pltpu.roll(here, 1, 1) + pltpu.roll(down * here, nz - 1, 1))
        )

    def send_y(e, y, plane_value, value_s, value_n):
        pack_s[e] = value_s * inv_s[...]
        send(e, 2, pack_s.at[e])
        pack_n[e] = value_n * inv_n[...]
        send(e, 3, pack_n.at[e])
        for side, plane in ((0, 0), (1, nx - 1)):
            y[plane + 1] = plane_value(plane) * inv[plane]
            send(e, side, y.at[plane + 1])

    def gained(scale, e):
        return (
            lambda s: (scale * gain_x[s]) * halo_x[e, s],
            lambda s: (scale * gain_y[s]) * halo_y[e, s],
        )

    def composite(c, e, between, image, image_of=lambda i, value: value, scale=lambda: -1.0):
        y, first, second = ys.at[c], firsts.at[c], seconds.at[c]

        def step_first(i, _):
            value = own_first * y[i + 1] + near_first * (inv[i] * near(y, i))
            first[i + 1] = value
            pack_s[e + 1, pl.ds(i, 1), :] = value[0:1]
            pack_n[e + 1, pl.ds(i, 1), :] = value[ny - 1 : ny]

        loop(0, nx, step_first)
        row_s, row_n = pack_s.at[e + 1], pack_n.at[e + 1]
        settle(e, first, 1, row_s, row_n, *gained(near_first, e), e + 1)
        scatter(first, 1, row_s, row_n)
        between(0)

        def step_second(i, _):
            value = own_second * first[i + 1] + base_second * y[i + 1] + push_second * (inv[i] * near(first, i))
            second[i + 1] = value
            pack_s[e + 2, pl.ds(i, 1), :] = value[0:1]
            pack_n[e + 2, pl.ds(i, 1), :] = value[ny - 1 : ny]

        loop(0, nx, step_second)
        row_s2, row_n2 = pack_s.at[e + 2], pack_n.at[e + 2]
        settle(e + 1, second, 1, row_s2, row_n2, *gained(push_second, e + 1), e + 2)
        scatter(second, 1, row_s2, row_n2)
        between(1)

        def step_image(i, _):
            value = image_of(i, diag[i] * second[i + 1] - near(second, i))
            image[i] = value
            side_s[c, pl.ds(i, 1), :] = value[0:1]
            side_n[c, pl.ds(i, 1), :] = value[ny - 1 : ny]

        loop(0, nx, step_image)
        settle(
            e + 2, image, 0, side_s.at[c], side_n.at[c],
            lambda s: scale() * (face_x[s] * halo_x[e + 2, s]),
            lambda s: scale() * (face_y[s] * halo_y[e + 2, s]),
        )

    def reduce_start(buffer, axis, position, count, send_sems, recv_sems):
        for k in range(1, count):
            reduce_copy(buffer, axis, position, count, k, send_sems, recv_sems).start()

    def reduce_copy(buffer, axis, position, count, k, send_sems, recv_sems):
        return pltpu.make_async_remote_copy(
            src_ref=buffer.at[0],
            dst_ref=buffer.at[k],
            send_sem=send_sems.at[k],
            recv_sem=recv_sems.at[k],
            device_id={axis: lax.rem(position + k, count)},
            device_id_type=MESH,
        )

    def reduce_end(buffer, axis, position, count, send_sems, recv_sems):
        value = buffer[0]
        for k in range(1, count):
            reduce_copy(buffer, axis, position, count, k, send_sems, recv_sems).wait()
            value = value + buffer[k]
        return value

    def over_x(t):
        return red_x.at[t], "gx", gx, ngx, rx_send.at[t], rx_recv.at[t]

    def over_y(t):
        return red_y.at[t], "gy", gy, ngy, ry_send.at[t], ry_recv.at[t]

    def put_sums(t, sums):
        red_x[t, 0, 0:8, :] = sums[0]
        red_x[t, 0, 8:16, :] = sums[1]
        reduce_start(*over_x(t))

    def relay(t):
        red_y[t, 0] = reduce_end(*over_x(t))
        reduce_start(*over_y(t))

    def take_sums(t):
        both = reduce_end(*over_y(t))
        return total(both[0:8]), total(both[8:16])

    send_y(1, ys.at[0], lambda p: right_ref[p], side_s[4], side_n[4])
    scatter(diag, 0, ds_, dn_)

    def start_plane(i, _):
        value = 1.0 / diag[i]
        inv[i] = value
        ys[0, i + 1] = right_ref[i] * value

    loop(1, nx - 1, start_plane)
    composite(0, 1, lambda k: None, images.at[0])

    w0, u0 = images.at[0], seconds.at[0]
    send_y(4, ys.at[1], lambda p: w0[p], side_s[0], side_n[0])
    scatter(w0, 0, side_s.at[0], side_n.at[0])
    tile = jnp.zeros((8, 128), jnp.float32)

    def second_plane(i, sums):
        w = w0[i]
        u = u0[i + 1]
        ys[1, i + 1] = w * inv[i]
        return sums[0] + fold(right_ref[i] * u), sums[1] + fold(w * u)

    sums = (tile, tile)
    for plane in (0, nx - 1):
        u = u0[plane + 1]
        sums = (sums[0] + fold(right_ref[plane] * u), sums[1] + fold(w0[plane] * u))
    put_sums(0, loop(1, nx - 1, second_plane, sums))
    composite(1, 4, lambda k: relay(0) if k == 0 else None, images.at[1])
    g0, h0 = take_sums(0)
    a0 = g0 / h0

    m0, n0 = seconds.at[1], images.at[1]
    for plane in (0, nx - 1):
        w_next[plane] = w0[plane] - a0 * n0[plane]
    send_y(7, ys.at[2], lambda p: w_next[p], side_s[0] - a0 * side_s[1], side_n[0] - a0 * side_n[1])
    scatter(n0, 0, side_s.at[1], side_n.at[1])

    def advance(i, sums):
        w = w_next[i]
        r = right_ref[i] - a0 * w0[i]
        u = u0[i + 1] - a0 * m0[i + 1]
        return sums[0] + fold(r * u), sums[1] + fold(w * u)

    def third_plane(i, sums):
        w = w0[i] - a0 * n0[i]
        w_next[i] = w
        ys[2, i + 1] = w * inv[i]
        return advance(i, sums)

    sums = (tile, tile)
    for plane in (0, nx - 1):
        sums = advance(plane, sums)
    put_sums(1, loop(1, nx - 1, third_plane, sums))
    found = []

    def last_between(k):
        if k == 0:
            relay(1)
            return
        g1, h1 = take_sums(1)
        b = g1 / g0
        a1 = g1 / (h1 - b * g1 / a0)
        found.extend((a1, b))

        def finish(i, _):
            u, m = u0[i + 1], m0[i + 1]
            u_next = u - a0 * m
            x_out[i] = a0 * u + a1 * (u_next + b * u)
            u_out[i] = u_next - a1 * (seconds[2, i + 1] + b * m)
            w = w0[i]
            r_out[i] = (right_ref[i] - a0 * w) - a1 * (w_next[i] + b * w)

        loop(0, nx, finish)

    composite(
        2, 7, last_between, w_out,
        lambda i, value: w_next[i] - found[0] * (value + found[1] * n0[i]),
        lambda: found[0],
    )
    scatter(w_out, 0, side_s.at[2], side_n.at[2])

    for e, side, source in sent:
        pl.when(has[side])(functools.partial(lambda c: c.wait_send(), copy_of(e, side, source)))


def deliver(parts, *refs):
    held, outs, sems = refs[:4], refs[4:8], refs[8]
    span = held[0].shape[0] // parts
    copies = []
    for k in range(4):
        for p in range(parts):
            rows = pl.ds(p * span, span)
            copies.append(pltpu.make_async_copy(held[k].at[rows], outs[k].at[rows], sems.at[k, p]))
            copies[-1].start()
    for copy in copies:
        copy.wait()


def solution(mesh):
    ngx, ngy = mesh.shape["gx"], mesh.shape["gy"]

    def local(right_side, phase, table):
        nx, ny, nz = right_side.shape
        f32 = jnp.float32
        block = pltpu.VMEM((nx, ny, nz), f32)
        three = pltpu.VMEM((3, nx + 2, ny, nz), f32)
        packed = pltpu.VMEM((EXCHANGES, nx, nz), f32)
        packed_one = pltpu.VMEM((nx, nz), f32)
        sides = pltpu.VMEM((5, nx, nz), f32)
        whole = pl.BlockSpec(memory_space=pltpu.VMEM)
        far = pl.BlockSpec(memory_space=pltpu.HBM)
        held = pl.pallas_call(
            functools.partial(kernel, ngx, ngy),
            out_shape=[block] * 4,
            in_specs=[far] * 3,
            out_specs=[whole] * 4,
            scratch_shapes=[
                block, pltpu.VMEM((nx, ny, nz), jnp.int32), pltpu.SMEM(table.shape, f32),
                three, pltpu.VMEM((2, nx, ny, nz), f32),
                block, pltpu.VMEM((nx + 1, ny, nz), f32), block, block, block, block,
                three, three, block,
                packed, packed, packed_one, packed_one, sides, sides,
                pltpu.VMEM((2, ny, nz), f32), pltpu.VMEM((2, nx, nz), f32),
                pltpu.VMEM((2, ny, nz), f32), pltpu.VMEM((2, nx, nz), f32),
                pltpu.VMEM((EXCHANGES, 2, ny, nz), f32), pltpu.VMEM((EXCHANGES, 2, nx, nz), f32),
                pltpu.VMEM((2, ngx, 16, 128), f32), pltpu.VMEM((2, ngy, 16, 128), f32),
                pltpu.SemaphoreType.DMA((EXCHANGES, 4)), pltpu.SemaphoreType.DMA((EXCHANGES, 4)),
                pltpu.SemaphoreType.DMA((2, ngx)), pltpu.SemaphoreType.DMA((2, ngx)),
                pltpu.SemaphoreType.DMA((2, ngy)), pltpu.SemaphoreType.DMA((2, ngy)),
                pltpu.SemaphoreType.DMA((6,)),
            ],
            compiler_params=pltpu.CompilerParams(
                collective_id=0, has_side_effects=True, vmem_limit_bytes=59 * 1024 * 1024 + 512 * 1024
            ),
        )(right_side, phase, table)
        parts = next(p for p in (2, 1) if nx % p == 0)
        return pl.pallas_call(
            functools.partial(deliver, parts),
            out_shape=[jax.ShapeDtypeStruct((nx, ny, nz), f32)] * 4,
            in_specs=[whole] * 4,
            out_specs=[far] * 4,
            scratch_shapes=[pltpu.SemaphoreType.DMA((4, parts))],
            compiler_params=pltpu.CompilerParams(vmem_limit_bytes=16 * 1024 * 1024),
        )(*held)

    spec = P("gx", "gy", None)
    return jax.shard_map(
        local, mesh=mesh, in_specs=(spec, spec, P()), out_specs=(spec,) * 4, check_vma=False
    )
```

```python
import functools

import jax
import jax.numpy as jnp
from jax import lax
from jax.experimental import pallas as pl
from jax.experimental.pallas import tpu as pltpu
from jax.sharding import PartitionSpec as P

MESH = pl.DeviceIdType.MESH

centre_value = 1.1
half_width = 0.9
ratio_sigma = centre_value / half_width
rho_first = 1.0 / ratio_sigma
rho_second = 1.0 / (2.0 * ratio_sigma - rho_first)
rho_third = 1.0 / (2.0 * ratio_sigma - rho_second)
start_scale = 1.0 / centre_value
keep_first = rho_second * rho_first
push_first = 2.0 * rho_second / half_width
keep_second = rho_third * rho_second
push_second = 2.0 * rho_third / half_width

own_first = start_scale * (1.0 + keep_first) + push_first * (1.0 - start_scale)
near_first = push_first * start_scale
own_second = 1.0 + keep_second - push_second
base_second = push_second - keep_second * start_scale

EXCHANGES = 11
SCALES = 10


def loop(low, high, body, carry=None):
    count = high - low
    unroll = next(u for u in (4, 5, 3, 2, 1) if count % u == 0)

    def step(k, value):
        for j in range(unroll):
            value = body(low + k * unroll + j, value)
        return value

    return lax.fori_loop(0, count // unroll, step, carry)


def fold(block):
    rows, lanes = block.shape
    tile = block[0:8]
    for k in range(1, rows // 8):
        tile = tile + block[8 * k : 8 * k + 8]
    out = tile[:, 0:128]
    for k in range(1, lanes // 128):
        out = out + tile[:, 128 * k : 128 * k + 128]
    return out


def total(tile):
    return jnp.sum(jnp.sum(tile, axis=0, keepdims=True), axis=1, keepdims=True)


def kernel(
    ngx, ngy,
    right_in, phase_in, table_in,
    x_out, r_out, u_out, w_out,
    right_ref, phase_ref, table_ref,
    seconds, n0,
    rho, cx, cs, cd, root, scale,
    ys, firsts,
    pack_s, pack_n, side_s, side_n,
    face_x, face_y, gain_x, gain_y,
    halo_x, halo_y, red_x, red_y,
    send_sem, recv_sem, rx_send, rx_recv, ry_send, ry_recv, in_sem,
):
    nx, ny, nz = right_ref.shape
    gx = lax.axis_index("gx")
    gy = lax.axis_index("gy")
    has = (gx > 0, gx < ngx - 1, gy > 0, gy < ngy - 1)

    parts = next(p for p in (4, 2, 1) if nx % p == 0)
    span = nx // parts
    fetch_table = pltpu.make_async_copy(table_in, table_ref, in_sem.at[parts + 1])
    fetch_table.start()
    fetches = []
    for p in range(parts):
        rows = pl.ds(p * span, span)
        fetches.append(pltpu.make_async_copy(phase_in.at[rows], phase_ref.at[rows], in_sem.at[p]))
        fetches[p].start()
    fetch_right = pltpu.make_async_copy(right_in, right_ref, in_sem.at[parts])
    fetch_right.start()

    barrier = pltpu.get_barrier_semaphore()
    for k in range(1, ngx):
        pl.semaphore_signal(barrier, inc=1, device_id={"gx": lax.rem(gx + k, ngx)}, device_id_type=MESH)
    for k in range(1, ngy):
        pl.semaphore_signal(barrier, inc=1, device_id={"gy": lax.rem(gy + k, ngy)}, device_id_type=MESH)

    def halo(e, side):
        return halo_x.at[e, side] if side < 2 else halo_y.at[e, side - 2]

    def copy_of(e, side, src):
        axis, position = ("gx", gx) if side < 2 else ("gy", gy)
        step = -1 if side % 2 == 0 else 1
        return pltpu.make_async_remote_copy(
            src_ref=src,
            dst_ref=halo(e, side ^ 1),
            send_sem=send_sem.at[e, side],
            recv_sem=recv_sem.at[e, side ^ 1],
            device_id={axis: position + step},
            device_id_type=MESH,
        )

    sent = []

    def send(e, side, source):
        pl.when(has[side])(functools.partial(lambda c: c.start(), copy_of(e, side, source)))
        sent.append((e, side, source))

    def arrive(e, sides):
        for side in sides:
            dummy = pltpu.make_async_remote_copy(
                src_ref=halo(e, side),
                dst_ref=halo(e, side),
                send_sem=send_sem.at[e, side],
                recv_sem=recv_sem.at[e, side],
                device_id={"gx": gx, "gy": gy},
                device_id_type=MESH,
            )
            pl.when(has[side])(functools.partial(lambda c: c.wait_recv(), dummy))

    fetch_table.wait()

    t1, t2, t3 = (jnp.full((1, 1), table_ref[k], jnp.float32) for k in (1, 2, 3))
    q0 = 1.0 / jnp.full((1, 1), table_ref[0], jnp.float32)
    q1, q2, q3 = 1.0 / t1, 1.0 / t2, 1.0 / t3

    for side in range(4):
        def outside(side=side):
            for e in range(EXCHANGES):
                target = halo(e, side)
                fill = jnp.zeros(target.shape, jnp.float32)
                target[...] = fill + q0 if e == 0 else fill

        pl.when(jnp.logical_not(has[side]))(outside)

    def lookup_plane(i, _):
        labels = phase_ref[i]
        value = jnp.where(labels == 1, q1, jnp.where(labels == 2, q2, jnp.where(labels == 3, q3, q0)))
        rho[i] = value
        pack_s[0, pl.ds(i, 1), :] = value[0:1]
        pack_n[0, pl.ds(i, 1), :] = value[ny - 1 : ny]

    for p in range(parts):
        fetches[p].wait()
        loop(p * span, (p + 1) * span, lookup_plane)
    pl.semaphore_wait(barrier, ngx - 1 + ngy - 1)
    send(0, 2, pack_s.at[0])
    send(0, 3, pack_n.at[0])
    send(0, 0, rho.at[0])
    send(0, 1, rho.at[nx - 1])

    row = lax.broadcasted_iota(jnp.int32, (ny, nz), 0)
    lane = lax.broadcasted_iota(jnp.int32, (ny, nz), 1)
    zero = jnp.zeros((ny, nz), jnp.float32)
    cx[0] = zero
    cx[nx] = zero
    for c in range(3):
        for buffer in (ys, firsts, seconds):
            buffer[c, 0] = zero
            buffer[c, nx + 1] = zero

    def couple_x(i, _):
        cx[i] = 2.0 / (rho[i - 1] + rho[i])

    loop(1, nx, couple_x)
    fetch_right.wait()

    def right_rows(i, _):
        right = right_ref[i]
        side_s[4, pl.ds(i, 1), :] = right[0:1]
        side_n[4, pl.ds(i, 1), :] = right[ny - 1 : ny]

    loop(0, nx, right_rows)

    def couple_rest(i, _):
        here = rho[i]
        south = jnp.where(row == 0, 0.0, 2.0 / (here + pltpu.roll(here, 1, 0)))
        beside = jnp.where(lane == 0, q0, pltpu.roll(here, 1, 1))
        down = 2.0 / (here + beside)
        last = 2.0 / (here[:, nz - 128 :] + q0)
        last = jnp.concatenate([jnp.zeros((ny, nz - 128), jnp.float32), last], axis=1)
        inner = jnp.where(lane == 0, 0.0, down)
        cs[i] = south
        cd[i] = inner
        up = jnp.where(lane == nz - 1, last, pltpu.roll(inner, nz - 1, 1))
        d = cx[i] + cx[i + 1] + south + pltpu.roll(south, ny - 1, 0) + down + up
        root[i] = d
        side_s[3, pl.ds(i, 1), :] = d[0:1]
        side_n[3, pl.ds(i, 1), :] = d[ny - 1 : ny]

    loop(0, nx, couple_rest)

    def scatter(ref, first, row_s, row_n):
        def one(i, _):
            ref[first + i, 0:1, :] = row_s[pl.ds(i, 1), :]
            ref[first + i, ny - 1 : ny, :] = row_n[pl.ds(i, 1), :]

        loop(1, nx - 1, one)

    def settle(e, ref, first, row_s, row_n, add_x, add_y, e_out=None):
        edge = (first, first + nx - 1)
        arrive(e, (0, 1))
        for side, i in ((0, 0), (1, nx - 1)):
            plane = ref[edge[side]] + add_x(side)
            ref[edge[side]] = plane
            row_s[i : i + 1, :] = plane[0:1]
            row_n[i : i + 1, :] = plane[ny - 1 : ny]
        for k, rows in ((0, row_s), (1, row_n)):
            arrive(e, (2 + k,))
            rows[...] = rows[...] + add_y(k)
            if e_out is not None:
                send(e_out, 2 + k, rows)
        for side, i in ((0, 0), (1, nx - 1)):
            ref[edge[side], 0:1, :] = row_s[i : i + 1, :]
            ref[edge[side], ny - 1 : ny, :] = row_n[i : i + 1, :]
            if e_out is not None:
                send(e_out, side, ref.at[edge[side]])

    arrive(0, range(4))
    for side, plane in ((0, 0), (1, nx - 1)):
        face_x[side] = 2.0 / (rho[plane] + halo_x[0, side])
    face_y[0] = 2.0 / (pack_s[0] + halo_y[0, 0])
    face_y[1] = 2.0 / (pack_n[0] + halo_y[0, 1])
    ds_, dn_ = side_s.at[3], side_n.at[3]
    for side, plane in ((0, 0), (1, nx - 1)):
        whole = root[plane] + face_x[side]
        root[plane] = whole
        ds_[plane : plane + 1, :] = whole[0:1]
        dn_[plane : plane + 1, :] = whole[ny - 1 : ny]
    ds_[...] = ds_[...] + face_y[0]
    dn_[...] = dn_[...] + face_y[1]
    for plane in (0, nx - 1):
        root[plane, 0:1, :] = ds_[plane : plane + 1, :]
        root[plane, ny - 1 : ny, :] = dn_[plane : plane + 1, :]

    def inverse_root(d):
        guess = lax.rsqrt(d)
        return guess * (1.5 - 0.5 * (d * guess) * guess)

    for k, (packed, rows) in enumerate(((pack_s, ds_), (pack_n, dn_))):
        packed[SCALES] = inverse_root(rows[...])
        send(SCALES, 2 + k, packed.at[SCALES])
    for side, plane in ((0, 0), (1, nx - 1)):
        scale[plane] = inverse_root(root[plane])
        send(SCALES, side, scale.at[plane])
    for k, (packed, rows) in enumerate(((pack_s, side_s), (pack_n, side_n))):
        packed[1] = rows[4] * packed[SCALES]
        send(1, 2 + k, packed.at[1])
    for side, plane in ((0, 0), (1, nx - 1)):
        ys[0, plane + 1] = right_ref[plane] * scale[plane]
        send(1, side, ys.at[0, plane + 1])
    scatter(root, 0, ds_, dn_)

    def scale_plane(i, _):
        d = root[i]
        value = inverse_root(d)
        scale[i] = value
        root[i] = d * value
        ys[0, i + 1] = right_ref[i] * value

    loop(1, nx - 1, scale_plane)
    for plane in (0, nx - 1):
        root[plane] = root[plane] * scale[plane]
    for rows, packed in ((ds_, pack_s), (dn_, pack_n)):
        rows[...] = rows[...] * packed[SCALES]

    def scale_couplings(i, _):
        here = scale[i]
        cx[i] = cx[i] * (here * scale[i - 1])
        cs[i] = cs[i] * (here * pltpu.roll(here, 1, 0))
        cd[i] = cd[i] * (here * pltpu.roll(here, 1, 1))

    here = scale[0]
    cs[0] = cs[0] * (here * pltpu.roll(here, 1, 0))
    cd[0] = cd[0] * (here * pltpu.roll(here, 1, 1))
    loop(1, nx, scale_couplings)

    def sweep(f, leave):
        unroll = next(u for u in (4, 2, 1) if nx % u == 0)

        def step(k, _):
            base = k * unroll
            west, here, to_west = f[base], f[base + 1], cx[base]
            for j in range(unroll):
                i = base + j
                east, to_east, south, down = f[i + 2], cx[i + 1], cs[i], cd[i]
                near = (
                    (to_west * west + to_east * east)
                    + (south * pltpu.roll(here, 1, 0) + pltpu.roll(south * here, ny - 1, 0))
                    + (down * pltpu.roll(here, 1, 1) + pltpu.roll(down * here, nz - 1, 1))
                )
                leave(i, here, near)
                west, here, to_west = here, east, to_east

        lax.fori_loop(0, nx // unroll, step, None)

    def gained(factor, e):
        return (
            lambda s: (factor * gain_x[s]) * halo_x[e, s],
            lambda s: (factor * gain_y[s]) * halo_y[e, s],
        )

    def put_rows(rows_s, rows_n, i, value):
        rows_s[pl.ds(i, 1), :] = value[0:1]
        rows_n[pl.ds(i, 1), :] = value[ny - 1 : ny]

    def composite(c, e, between, image, image_first, rows, adds, image_of=lambda i, value: value, e_out=None):
        v, first, second = ys.at[c], firsts.at[c], seconds.at[c]
        rows_1 = pack_s.at[e + 1], pack_n.at[e + 1]
        rows_2 = pack_s.at[e + 2], pack_n.at[e + 2]

        def leave_first(i, here, near):
            value = own_first * here + near_first * near
            first[i + 1] = value
            put_rows(*rows_1, i, value)

        sweep(v, leave_first)
        if c == 0:
            arrive(SCALES, range(4))
            for side, plane in ((0, 0), (1, nx - 1)):
                gain_x[side] = (face_x[side] * scale[plane]) * halo_x[SCALES, side]
            gain_y[0] = (face_y[0] * pack_s[SCALES]) * halo_y[SCALES, 0]
            gain_y[1] = (face_y[1] * pack_n[SCALES]) * halo_y[SCALES, 1]
        settle(e, first, 1, *rows_1, *gained(near_first, e), e + 1)
        scatter(first, 1, *rows_1)
        between(0)

        def leave_second(i, here, near):
            value = own_second * here + (base_second * v[i + 1] + push_second * near)
            second[i + 1] = value
            put_rows(*rows_2, i, value)

        sweep(first, leave_second)
        settle(e + 1, second, 1, *rows_2, *gained(push_second, e + 1), e + 2)
        scatter(second, 1, *rows_2)
        between(1)

        def leave_image(i, here, near):
            value = image_of(i, here - near)
            image[image_first + i] = value
            put_rows(*rows, i, value)

        sweep(second, leave_image)
        settle(e + 2, image, image_first, *rows, *adds(e + 2), e_out)
        scatter(image, image_first, *rows)

    def reduce_start(buffer, axis, position, count, send_sems, recv_sems):
        for k in range(1, count):
            reduce_copy(buffer, axis, position, count, k, send_sems, recv_sems).start()

    def reduce_copy(buffer, axis, position, count, k, send_sems, recv_sems):
        return pltpu.make_async_remote_copy(
            src_ref=buffer.at[0],
            dst_ref=buffer.at[k],
            send_sem=send_sems.at[k],
            recv_sem=recv_sems.at[k],
            device_id={axis: lax.rem(position + k, count)},
            device_id_type=MESH,
        )

    def reduce_end(buffer, axis, position, count, send_sems, recv_sems):
        value = buffer[0]
        for k in range(1, count):
            reduce_copy(buffer, axis, position, count, k, send_sems, recv_sems).wait()
            value = value + buffer[k]
        return value

    def over_x(t):
        return red_x.at[t], "gx", gx, ngx, rx_send.at[t], rx_recv.at[t]

    def over_y(t):
        return red_y.at[t], "gy", gy, ngy, ry_send.at[t], ry_recv.at[t]

    def put_sums(t, sums):
        red_x[t, 0, 0:8, :] = sums[0]
        red_x[t, 0, 8:16, :] = sums[1]
        reduce_start(*over_x(t))

    def relay(t):
        red_y[t, 0] = reduce_end(*over_x(t))
        reduce_start(*over_y(t))

    def take_sums(t):
        both = reduce_end(*over_y(t))
        return total(both[0:8]), total(both[8:16])

    def less(e):
        return gained(-1.0, e)

    composite(0, 1, lambda k: None, ys.at[1], 1, (pack_s.at[4], pack_n.at[4]), less, e_out=4)

    r0, w0, w1 = ys.at[0], ys.at[1], ys.at[2]
    u0, m0 = seconds.at[0], seconds.at[1]
    tile = jnp.zeros((8, 128), jnp.float32)

    def first_sums(i, sums):
        u = u0[i + 1]
        return sums[0] + fold(r0[i + 1] * u), sums[1] + fold(w0[i + 1] * u)

    put_sums(0, loop(0, nx, first_sums, (tile, tile)))
    composite(
        1, 4, lambda k: relay(0) if k == 0 else None, n0, 0, (side_s.at[1], side_n.at[1]), less
    )
    g0, h0 = take_sums(0)
    a0 = g0 / h0

    for k, (packed, rows) in enumerate(((pack_s, side_s), (pack_n, side_n))):
        packed[7] = packed[4] - a0 * rows[1]
        send(7, 2 + k, packed.at[7])
    for side, plane in ((0, 0), (1, nx - 1)):
        w1[plane + 1] = w0[plane + 1] - a0 * n0[plane]
        send(7, side, w1.at[plane + 1])

    def advance(i, sums, w):
        r = r0[i + 1] - a0 * w0[i + 1]
        u = u0[i + 1] - a0 * m0[i + 1]
        return sums[0] + fold(r * u), sums[1] + fold(w * u)

    def second_sums(i, sums):
        w = w0[i + 1] - a0 * n0[i]
        w1[i + 1] = w
        return advance(i, sums, w)

    sums = (tile, tile)
    for plane in (0, nx - 1):
        sums = advance(plane, sums, w1[plane + 1])
    put_sums(1, loop(1, nx - 1, second_sums, sums))
    found = []

    def last_between(k):
        if k == 0:
            relay(1)
            return
        g1, h1 = take_sums(1)
        b = g1 / g0
        a1 = g1 / (h1 - b * g1 / a0)
        found.extend((a1, b))

        def finish(i, _):
            u, m, w, part = u0[i + 1], m0[i + 1], w0[i + 1], scale[i]
            u1 = u - a0 * m
            x_out[i] = part * (a0 * u + a1 * (u1 + b * u))
            u_out[i] = part * (u1 - a1 * (seconds[2, i + 1] + b * m))
            r_out[i] = right_ref[i] - root[i] * (a0 * w + a1 * (w1[i + 1] + b * w))

        loop(0, nx, finish)

    def last_adds(e):
        return (
            lambda s: (found[0] * root[(0, nx - 1)[s]]) * (gain_x[s] * halo_x[e, s]),
            lambda s: (found[0] * (ds_, dn_)[s][...]) * (gain_y[s] * halo_y[e, s]),
        )

    composite(
        2, 7, last_between, w_out, 0, (side_s.at[2], side_n.at[2]), last_adds,
        lambda i, value: root[i] * (w1[i + 1] - found[0] * (value + found[1] * n0[i])),
    )

    for e, side, source in sent:
        pl.when(has[side])(functools.partial(lambda c: c.wait_send(), copy_of(e, side, source)))


def deliver(parts, *refs):
    held, outs, sems = refs[:4], refs[4:8], refs[8]
    span = held[0].shape[0] // parts
    copies = []
    for k in range(4):
        for p in range(parts):
            rows = pl.ds(p * span, span)
            copies.append(pltpu.make_async_copy(held[k].at[rows], outs[k].at[rows], sems.at[k, p]))
            copies[-1].start()
    for copy in copies:
        copy.wait()


def solution(mesh):
    ngx, ngy = mesh.shape["gx"], mesh.shape["gy"]

    def local(right_side, phase, table):
        nx, ny, nz = right_side.shape
        f32 = jnp.float32
        block = pltpu.VMEM((nx, ny, nz), f32)
        three = pltpu.VMEM((3, nx + 2, ny, nz), f32)
        packed = pltpu.VMEM((EXCHANGES, nx, nz), f32)
        sides = pltpu.VMEM((5, nx, nz), f32)
        whole = pl.BlockSpec(memory_space=pltpu.VMEM)
        far = pl.BlockSpec(memory_space=pltpu.HBM)
        held = pl.pallas_call(
            functools.partial(kernel, ngx, ngy),
            out_shape=[block] * 4,
            in_specs=[far] * 3,
            out_specs=[whole] * 4,
            scratch_shapes=[
                block, pltpu.VMEM((nx, ny, nz), jnp.int32), pltpu.SMEM(table.shape, f32),
                three, block,
                block, pltpu.VMEM((nx + 1, ny, nz), f32), block, block, block, block,
                three, three,
                packed, packed, sides, sides,
                pltpu.VMEM((2, ny, nz), f32), pltpu.VMEM((2, nx, nz), f32),
                pltpu.VMEM((2, ny, nz), f32), pltpu.VMEM((2, nx, nz), f32),
                pltpu.VMEM((EXCHANGES, 2, ny, nz), f32), pltpu.VMEM((EXCHANGES, 2, nx, nz), f32),
                pltpu.VMEM((2, ngx, 16, 128), f32), pltpu.VMEM((2, ngy, 16, 128), f32),
                pltpu.SemaphoreType.DMA((EXCHANGES, 4)), pltpu.SemaphoreType.DMA((EXCHANGES, 4)),
                pltpu.SemaphoreType.DMA((2, ngx)), pltpu.SemaphoreType.DMA((2, ngx)),
                pltpu.SemaphoreType.DMA((2, ngy)), pltpu.SemaphoreType.DMA((2, ngy)),
                pltpu.SemaphoreType.DMA((6,)),
            ],
            compiler_params=pltpu.CompilerParams(
                collective_id=0, has_side_effects=True, vmem_limit_bytes=59 * 1024 * 1024 + 512 * 1024
            ),
        )(right_side, phase, table)
        parts = next(p for p in (2, 1) if nx % p == 0)
        return pl.pallas_call(
            functools.partial(deliver, parts),
            out_shape=[jax.ShapeDtypeStruct((nx, ny, nz), f32)] * 4,
            in_specs=[whole] * 4,
            out_specs=[far] * 4,
            scratch_shapes=[pltpu.SemaphoreType.DMA((4, parts))],
            compiler_params=pltpu.CompilerParams(vmem_limit_bytes=16 * 1024 * 1024),
        )(*held)

    spec = P("gx", "gy", None)
    return jax.shard_map(
        local, mesh=mesh, in_specs=(spec, spec, P()), out_specs=(spec,) * 4, check_vma=False
    )
```

```python
import functools

import jax
import jax.numpy as jnp
from jax import lax
from jax.experimental import pallas as pl
from jax.experimental.pallas import tpu as pltpu
from jax.sharding import PartitionSpec as P

MESH = pl.DeviceIdType.MESH

centre_value = 1.1
half_width = 0.9
ratio_sigma = centre_value / half_width
rho_first = 1.0 / ratio_sigma
rho_second = 1.0 / (2.0 * ratio_sigma - rho_first)
rho_third = 1.0 / (2.0 * ratio_sigma - rho_second)
start_scale = 1.0 / centre_value
keep_first = rho_second * rho_first
push_first = 2.0 * rho_second / half_width
keep_second = rho_third * rho_second
push_second = 2.0 * rho_third / half_width

own_first = start_scale * (1.0 + keep_first) + push_first * (1.0 - start_scale)
near_first = push_first * start_scale
own_second = 1.0 + keep_second - push_second
base_second = push_second - keep_second * start_scale

EXCHANGES = 10


def loop(low, high, body, carry=None):
    count = high - low
    unroll = next(u for u in (4, 5, 3, 2, 1) if count % u == 0)

    def step(k, value):
        for j in range(unroll):
            value = body(low + k * unroll + j, value)
        return value

    return lax.fori_loop(0, count // unroll, step, carry)


def fold(block):
    rows, lanes = block.shape
    tile = block[0:8]
    for k in range(1, rows // 8):
        tile = tile + block[8 * k : 8 * k + 8]
    out = tile[:, 0:128]
    for k in range(1, lanes // 128):
        out = out + tile[:, 128 * k : 128 * k + 128]
    return out


def total(tile):
    return jnp.sum(jnp.sum(tile, axis=0, keepdims=True), axis=1, keepdims=True)


def kernel(
    ngx, ngy,
    right_in, phase_in, table_in,
    x_out, r_out, u_out, w_out,
    right_ref, phase_ref, table_ref,
    seconds, images,
    rho, cx, cs, cd, diag, inv,
    ys, firsts, w_next,
    pack_s, pack_n, inv_s, inv_n, side_s, side_n,
    face_x, face_y, gain_x, gain_y,
    halo_x, halo_y, red_x, red_y,
    send_sem, recv_sem, rx_send, rx_recv, ry_send, ry_recv, in_sem,
):
    nx, ny, nz = right_ref.shape
    gx = lax.axis_index("gx")
    gy = lax.axis_index("gy")
    has = (gx > 0, gx < ngx - 1, gy > 0, gy < ngy - 1)

    parts = next(p for p in (4, 2, 1) if nx % p == 0)
    span = nx // parts
    fetch_table = pltpu.make_async_copy(table_in, table_ref, in_sem.at[parts + 1])
    fetch_table.start()
    fetches = []
    for p in range(parts):
        rows = pl.ds(p * span, span)
        fetches.append(pltpu.make_async_copy(phase_in.at[rows], phase_ref.at[rows], in_sem.at[p]))
        fetches[p].start()
    fetch_right = pltpu.make_async_copy(right_in, right_ref, in_sem.at[parts])
    fetch_right.start()

    barrier = pltpu.get_barrier_semaphore()
    for k in range(1, ngx):
        pl.semaphore_signal(barrier, inc=1, device_id={"gx": lax.rem(gx + k, ngx)}, device_id_type=MESH)
    for k in range(1, ngy):
        pl.semaphore_signal(barrier, inc=1, device_id={"gy": lax.rem(gy + k, ngy)}, device_id_type=MESH)

    halves = 2 if nx % 16 == 0 else 1
    half = nx // halves
    pieces = {side: (None,) if side < 2 else tuple(range(halves)) for side in range(4)}

    def piece_of(ref, piece):
        return ref if piece is None else ref.at[pl.ds(piece * half, half)]

    def slot(side, piece):
        return side if piece is None else 2 + 2 * (side - 2) + piece

    def halo(e, side):
        return halo_x.at[e, side] if side < 2 else halo_y.at[e, side - 2]

    def copy_of(e, side, piece, src):
        axis, position = ("gx", gx) if side < 2 else ("gy", gy)
        step = -1 if side % 2 == 0 else 1
        return pltpu.make_async_remote_copy(
            src_ref=piece_of(src, piece),
            dst_ref=piece_of(halo(e, side ^ 1), piece),
            send_sem=send_sem.at[e, slot(side, piece)],
            recv_sem=recv_sem.at[e, slot(side ^ 1, piece)],
            device_id={axis: position + step},
            device_id_type=MESH,
        )

    sent = []

    def send(e, side, source, chosen=None):
        for piece in pieces[side] if chosen is None else (chosen,):
            copy = copy_of(e, side, piece, source)
            pl.when(has[side])(functools.partial(lambda c: c.start(), copy))
            sent.append((side, copy))

    def arrive(e, sides, chosen=None):
        for side in sides:
            for piece in pieces[side] if chosen is None else (chosen,):
                here = piece_of(halo(e, side), piece)
                dummy = pltpu.make_async_remote_copy(
                    src_ref=here,
                    dst_ref=here,
                    send_sem=send_sem.at[e, slot(side, piece)],
                    recv_sem=recv_sem.at[e, slot(side, piece)],
                    device_id={"gx": gx, "gy": gy},
                    device_id_type=MESH,
                )
                pl.when(has[side])(functools.partial(lambda c: c.wait_recv(), dummy))

    fetch_table.wait()

    t1, t2, t3 = (jnp.full((1, 1), table_ref[k], jnp.float32) for k in (1, 2, 3))
    q0 = 1.0 / jnp.full((1, 1), table_ref[0], jnp.float32)
    q1, q2, q3 = 1.0 / t1, 1.0 / t2, 1.0 / t3

    for side in range(4):
        def outside(side=side):
            for e in range(EXCHANGES):
                target = halo(e, side)
                fill = jnp.zeros(target.shape, jnp.float32)
                target[...] = fill + q0 if e == 0 else fill

        pl.when(jnp.logical_not(has[side]))(outside)

    def lookup_plane(i, _):
        labels = phase_ref[i]
        value = jnp.where(labels == 1, q1, jnp.where(labels == 2, q2, jnp.where(labels == 3, q3, q0)))
        rho[i] = value
        pack_s[0, pl.ds(i, 1), :] = value[0:1]
        pack_n[0, pl.ds(i, 1), :] = value[ny - 1 : ny]

    for p in range(parts):
        fetches[p].wait()
        loop(p * span, (p + 1) * span, lookup_plane)
    pl.semaphore_wait(barrier, ngx - 1 + ngy - 1)
    send(0, 2, pack_s.at[0])
    send(0, 3, pack_n.at[0])
    send(0, 0, rho.at[0])
    send(0, 1, rho.at[nx - 1])

    row = lax.broadcasted_iota(jnp.int32, (ny, nz), 0)
    lane = lax.broadcasted_iota(jnp.int32, (ny, nz), 1)
    zero = jnp.zeros((ny, nz), jnp.float32)
    cx[0] = zero
    cx[nx] = zero
    for c in range(3):
        for buffer in (ys, firsts, seconds):
            buffer[c, 0] = zero
            buffer[c, nx + 1] = zero

    def couple_x(i, _):
        cx[i] = 2.0 / (rho[i - 1] + rho[i])

    loop(1, nx, couple_x)
    fetch_right.wait()

    def right_rows(i, _):
        right = right_ref[i]
        side_s[4, pl.ds(i, 1), :] = right[0:1]
        side_n[4, pl.ds(i, 1), :] = right[ny - 1 : ny]

    loop(0, nx, right_rows)

    def couple_rest(i, _):
        here = rho[i]
        south = jnp.where(row == 0, 0.0, 2.0 / (here + pltpu.roll(here, 1, 0)))
        beside = jnp.where(lane == 0, q0, pltpu.roll(here, 1, 1))
        down = 2.0 / (here + beside)
        last = 2.0 / (here[:, nz - 128 :] + q0)
        last = jnp.concatenate([jnp.zeros((ny, nz - 128), jnp.float32), last], axis=1)
        inner = jnp.where(lane == 0, 0.0, down)
        cs[i] = south
        cd[i] = inner
        up = jnp.where(lane == nz - 1, last, pltpu.roll(inner, nz - 1, 1))
        d = cx[i] + cx[i + 1] + south + pltpu.roll(south, ny - 1, 0) + down + up
        diag[i] = d
        side_s[3, pl.ds(i, 1), :] = d[0:1]
        side_n[3, pl.ds(i, 1), :] = d[ny - 1 : ny]

    loop(0, nx, couple_rest)

    def scatter(ref, first, row_s, row_n):
        def one(i, _):
            ref[first + i, 0:1, :] = row_s[pl.ds(i, 1), :]
            ref[first + i, ny - 1 : ny, :] = row_n[pl.ds(i, 1), :]

        loop(1, nx - 1, one)

    def settle(e, ref, first, row_s, row_n, add_x, add_y, e_out=None):
        edge = (first, first + nx - 1)
        arrive(e, (0, 1))
        for side, i in ((0, 0), (1, nx - 1)):
            plane = ref[edge[side]] + add_x(side)
            ref[edge[side]] = plane
            row_s[i : i + 1, :] = plane[0:1]
            row_n[i : i + 1, :] = plane[ny - 1 : ny]
        for k, rows in ((0, row_s), (1, row_n)):
            for piece in pieces[2 + k]:
                arrive(e, (2 + k,), piece)
                part = slice(piece * half, (piece + 1) * half)
                rows[part] = rows[part] + add_y(k, part)
                if e_out is not None:
                    send(e_out, 2 + k, rows, piece)
        for side, i in ((0, 0), (1, nx - 1)):
            ref[edge[side], 0:1, :] = row_s[i : i + 1, :]
            ref[edge[side], ny - 1 : ny, :] = row_n[i : i + 1, :]
            if e_out is not None:
                send(e_out, side, ref.at[edge[side]])

    arrive(0, range(4))
    for side, plane in ((0, 0), (1, nx - 1)):
        face_x[side] = 2.0 / (rho[plane] + halo_x[0, side])
    face_y[0] = 2.0 / (pack_s[0] + halo_y[0, 0])
    face_y[1] = 2.0 / (pack_n[0] + halo_y[0, 1])
    ds_, dn_ = side_s.at[3], side_n.at[3]
    for side, plane in ((0, 0), (1, nx - 1)):
        whole = diag[plane] + face_x[side]
        diag[plane] = whole
        ds_[plane : plane + 1, :] = whole[0:1]
        dn_[plane : plane + 1, :] = whole[ny - 1 : ny]
    ds_[...] = ds_[...] + face_y[0]
    dn_[...] = dn_[...] + face_y[1]
    for plane in (0, nx - 1):
        diag[plane, 0:1, :] = ds_[plane : plane + 1, :]
        diag[plane, ny - 1 : ny, :] = dn_[plane : plane + 1, :]
    inv_s[...] = 1.0 / ds_[...]
    inv_n[...] = 1.0 / dn_[...]
    for side, plane in ((0, 0), (1, nx - 1)):
        inv[plane] = 1.0 / diag[plane]
        gain_x[side] = face_x[side] * inv[plane]
    gain_y[0] = face_y[0] * inv_s[...]
    gain_y[1] = face_y[1] * inv_n[...]

    def near(f, i):
        here = f[i + 1]
        south = cs[i]
        down = cd[i]
        return (
            (cx[i] * f[i] + cx[i + 1] * f[i + 2])
            + (south * pltpu.roll(here, 1, 0) + pltpu.roll(south * here, ny - 1, 0))
            + (down * pltpu.roll(here, 1, 1) + pltpu.roll(down * here, nz - 1, 1))
        )

    def send_y(e, y, plane_value, value_s, value_n):
        pack_s[e] = value_s * inv_s[...]
        send(e, 2, pack_s.at[e])
        pack_n[e] = value_n * inv_n[...]
        send(e, 3, pack_n.at[e])
        for side, plane in ((0, 0), (1, nx - 1)):
            y[plane + 1] = plane_value(plane) * inv[plane]
            send(e, side, y.at[plane + 1])

    def gained(scale, e):
        return (
            lambda s: (scale * gain_x[s]) * halo_x[e, s],
            lambda s, part: (scale * gain_y[s, part]) * halo_y[e, s, part],
        )

    def composite(c, e, between, image, image_of=lambda i, value: value, scale=lambda: -1.0):
        y, first, second = ys.at[c], firsts.at[c], seconds.at[c]

        def step_first(i, _):
            value = own_first * y[i + 1] + near_first * (inv[i] * near(y, i))
            first[i + 1] = value
            pack_s[e + 1, pl.ds(i, 1), :] = value[0:1]
            pack_n[e + 1, pl.ds(i, 1), :] = value[ny - 1 : ny]

        loop(0, nx, step_first)
        row_s, row_n = pack_s.at[e + 1], pack_n.at[e + 1]
        settle(e, first, 1, row_s, row_n, *gained(near_first, e), e + 1)
        scatter(first, 1, row_s, row_n)
        between(0)

        def step_second(i, _):
            value = own_second * first[i + 1] + base_second * y[i + 1] + push_second * (inv[i] * near(first, i))
            second[i + 1] = value
            pack_s[e + 2, pl.ds(i, 1), :] = value[0:1]
            pack_n[e + 2, pl.ds(i, 1), :] = value[ny - 1 : ny]

        loop(0, nx, step_second)
        row_s2, row_n2 = pack_s.at[e + 2], pack_n.at[e + 2]
        settle(e + 1, second, 1, row_s2, row_n2, *gained(push_second, e + 1), e + 2)
        scatter(second, 1, row_s2, row_n2)
        between(1)

        def step_image(i, _):
            value = image_of(i, diag[i] * second[i + 1] - near(second, i))
            image[i] = value
            side_s[c, pl.ds(i, 1), :] = value[0:1]
            side_n[c, pl.ds(i, 1), :] = value[ny - 1 : ny]

        loop(0, nx, step_image)
        settle(
            e + 2, image, 0, side_s.at[c], side_n.at[c],
            lambda s: scale() * (face_x[s] * halo_x[e + 2, s]),
            lambda s, part: scale() * (face_y[s, part] * halo_y[e + 2, s, part]),
        )

    def reduce_start(buffer, axis, position, count, send_sems, recv_sems):
        for k in range(1, count):
            reduce_copy(buffer, axis, position, count, k, send_sems, recv_sems).start()

    def reduce_copy(buffer, axis, position, count, k, send_sems, recv_sems):
        return pltpu.make_async_remote_copy(
            src_ref=buffer.at[0],
            dst_ref=buffer.at[k],
            send_sem=send_sems.at[k],
            recv_sem=recv_sems.at[k],
            device_id={axis: lax.rem(position + k, count)},
            device_id_type=MESH,
        )

    def reduce_end(buffer, axis, position, count, send_sems, recv_sems):
        value = buffer[0]
        for k in range(1, count):
            reduce_copy(buffer, axis, position, count, k, send_sems, recv_sems).wait()
            value = value + buffer[k]
        return value

    def over_x(t):
        return red_x.at[t], "gx", gx, ngx, rx_send.at[t], rx_recv.at[t]

    def over_y(t):
        return red_y.at[t], "gy", gy, ngy, ry_send.at[t], ry_recv.at[t]

    def put_sums(t, sums):
        red_x[t, 0, 0:8, :] = sums[0]
        red_x[t, 0, 8:16, :] = sums[1]
        reduce_start(*over_x(t))

    def relay(t):
        red_y[t, 0] = reduce_end(*over_x(t))
        reduce_start(*over_y(t))

    def take_sums(t):
        both = reduce_end(*over_y(t))
        return total(both[0:8]), total(both[8:16])

    send_y(1, ys.at[0], lambda p: right_ref[p], side_s[4], side_n[4])
    scatter(diag, 0, ds_, dn_)

    def start_plane(i, _):
        value = 1.0 / diag[i]
        inv[i] = value
        ys[0, i + 1] = right_ref[i] * value

    loop(1, nx - 1, start_plane)
    composite(0, 1, lambda k: None, images.at[0])

    w0, u0 = images.at[0], seconds.at[0]
    send_y(4, ys.at[1], lambda p: w0[p], side_s[0], side_n[0])
    scatter(w0, 0, side_s.at[0], side_n.at[0])
    tile = jnp.zeros((8, 128), jnp.float32)

    def second_plane(i, sums):
        w = w0[i]
        u = u0[i + 1]
        ys[1, i + 1] = w * inv[i]
        return sums[0] + fold(right_ref[i] * u), sums[1] + fold(w * u)

    sums = (tile, tile)
    for plane in (0, nx - 1):
        u = u0[plane + 1]
        sums = (sums[0] + fold(right_ref[plane] * u), sums[1] + fold(w0[plane] * u))
    put_sums(0, loop(1, nx - 1, second_plane, sums))
    composite(1, 4, lambda k: relay(0) if k == 0 else None, images.at[1])
    g0, h0 = take_sums(0)
    a0 = g0 / h0

    m0, n0 = seconds.at[1], images.at[1]
    for plane in (0, nx - 1):
        w_next[plane] = w0[plane] - a0 * n0[plane]
    send_y(7, ys.at[2], lambda p: w_next[p], side_s[0] - a0 * side_s[1], side_n[0] - a0 * side_n[1])
    scatter(n0, 0, side_s.at[1], side_n.at[1])

    def advance(i, sums):
        w = w_next[i]
        r = right_ref[i] - a0 * w0[i]
        u = u0[i + 1] - a0 * m0[i + 1]
        return sums[0] + fold(r * u), sums[1] + fold(w * u)

    def third_plane(i, sums):
        w = w0[i] - a0 * n0[i]
        w_next[i] = w
        ys[2, i + 1] = w * inv[i]
        return advance(i, sums)

    sums = (tile, tile)
    for plane in (0, nx - 1):
        sums = advance(plane, sums)
    put_sums(1, loop(1, nx - 1, third_plane, sums))
    found = []

    def last_between(k):
        if k == 0:
            relay(1)
            return
        g1, h1 = take_sums(1)
        b = g1 / g0
        a1 = g1 / (h1 - b * g1 / a0)
        found.extend((a1, b))

        def finish(i, _):
            u, m = u0[i + 1], m0[i + 1]
            u_next = u - a0 * m
            x_out[i] = a0 * u + a1 * (u_next + b * u)
            u_out[i] = u_next - a1 * (seconds[2, i + 1] + b * m)
            w = w0[i]
            r_out[i] = (right_ref[i] - a0 * w) - a1 * (w_next[i] + b * w)

        loop(0, nx, finish)

    composite(
        2, 7, last_between, w_out,
        lambda i, value: w_next[i] - found[0] * (value + found[1] * n0[i]),
        lambda: found[0],
    )
    scatter(w_out, 0, side_s.at[2], side_n.at[2])

    for side, copy in sent:
        pl.when(has[side])(functools.partial(lambda c: c.wait_send(), copy))


def deliver(parts, *refs):
    held, outs, sems = refs[:4], refs[4:8], refs[8]
    span = held[0].shape[0] // parts
    copies = []
    for k in range(4):
        for p in range(parts):
            rows = pl.ds(p * span, span)
            copies.append(pltpu.make_async_copy(held[k].at[rows], outs[k].at[rows], sems.at[k, p]))
            copies[-1].start()
    for copy in copies:
        copy.wait()


def solution(mesh):
    ngx, ngy = mesh.shape["gx"], mesh.shape["gy"]

    def local(right_side, phase, table):
        nx, ny, nz = right_side.shape
        f32 = jnp.float32
        block = pltpu.VMEM((nx, ny, nz), f32)
        three = pltpu.VMEM((3, nx + 2, ny, nz), f32)
        packed = pltpu.VMEM((EXCHANGES, nx, nz), f32)
        packed_one = pltpu.VMEM((nx, nz), f32)
        sides = pltpu.VMEM((5, nx, nz), f32)
        whole = pl.BlockSpec(memory_space=pltpu.VMEM)
        far = pl.BlockSpec(memory_space=pltpu.HBM)
        held = pl.pallas_call(
            functools.partial(kernel, ngx, ngy),
            out_shape=[block] * 4,
            in_specs=[far] * 3,
            out_specs=[whole] * 4,
            scratch_shapes=[
                block, pltpu.VMEM((nx, ny, nz), jnp.int32), pltpu.SMEM(table.shape, f32),
                three, pltpu.VMEM((2, nx, ny, nz), f32),
                block, pltpu.VMEM((nx + 1, ny, nz), f32), block, block, block, block,
                three, three, block,
                packed, packed, packed_one, packed_one, sides, sides,
                pltpu.VMEM((2, ny, nz), f32), pltpu.VMEM((2, nx, nz), f32),
                pltpu.VMEM((2, ny, nz), f32), pltpu.VMEM((2, nx, nz), f32),
                pltpu.VMEM((EXCHANGES, 2, ny, nz), f32), pltpu.VMEM((EXCHANGES, 2, nx, nz), f32),
                pltpu.VMEM((2, ngx, 16, 128), f32), pltpu.VMEM((2, ngy, 16, 128), f32),
                pltpu.SemaphoreType.DMA((EXCHANGES, 6)), pltpu.SemaphoreType.DMA((EXCHANGES, 6)),
                pltpu.SemaphoreType.DMA((2, ngx)), pltpu.SemaphoreType.DMA((2, ngx)),
                pltpu.SemaphoreType.DMA((2, ngy)), pltpu.SemaphoreType.DMA((2, ngy)),
                pltpu.SemaphoreType.DMA((6,)),
            ],
            compiler_params=pltpu.CompilerParams(
                collective_id=0, has_side_effects=True, vmem_limit_bytes=59 * 1024 * 1024 + 512 * 1024
            ),
        )(right_side, phase, table)
        parts = next(p for p in (2, 1) if nx % p == 0)
        return pl.pallas_call(
            functools.partial(deliver, parts),
            out_shape=[jax.ShapeDtypeStruct((nx, ny, nz), f32)] * 4,
            in_specs=[whole] * 4,
            out_specs=[far] * 4,
            scratch_shapes=[pltpu.SemaphoreType.DMA((4, parts))],
            compiler_params=pltpu.CompilerParams(vmem_limit_bytes=16 * 1024 * 1024),
        )(*held)

    spec = P("gx", "gy", None)
    return jax.shard_map(
        local, mesh=mesh, in_specs=(spec, spec, P()), out_specs=(spec,) * 4, check_vma=False
    )
```

```python
import functools

import jax
import jax.numpy as jnp
from jax import lax
from jax.experimental import pallas as pl
from jax.experimental.pallas import tpu as pltpu
from jax.sharding import PartitionSpec as P

MESH = pl.DeviceIdType.MESH

centre_value = 1.1
half_width = 0.9
ratio_sigma = centre_value / half_width
rho_first = 1.0 / ratio_sigma
rho_second = 1.0 / (2.0 * ratio_sigma - rho_first)
rho_third = 1.0 / (2.0 * ratio_sigma - rho_second)
start_scale = 1.0 / centre_value
keep_first = rho_second * rho_first
push_first = 2.0 * rho_second / half_width
keep_second = rho_third * rho_second
push_second = 2.0 * rho_third / half_width

own_first = start_scale * (1.0 + keep_first) + push_first * (1.0 - start_scale)
near_first = push_first * start_scale
own_second = 1.0 + keep_second - push_second
base_second = push_second - keep_second * start_scale

EXCHANGES = 10


def loop(low, high, body, carry=None):
    count = high - low
    unroll = next(u for u in (4, 5, 3, 2, 1) if count % u == 0)

    def step(k, value):
        for j in range(unroll):
            value = body(low + k * unroll + j, value)
        return value

    return lax.fori_loop(0, count // unroll, step, carry)


def fold(block):
    rows, lanes = block.shape
    tile = block[0:8]
    for k in range(1, rows // 8):
        tile = tile + block[8 * k : 8 * k + 8]
    out = tile[:, 0:128]
    for k in range(1, lanes // 128):
        out = out + tile[:, 128 * k : 128 * k + 128]
    return out


def total(row):
    return jnp.sum(row, axis=1, keepdims=True)


def kernel(
    ngx, ngy,
    right_in, phase_in, table_in,
    x_out, r_out, u_out, w_out,
    right_ref, phase_ref, table_ref,
    seconds, images,
    rho, cx, cs, cd, diag, inv,
    ys, firsts, w_next,
    pack_s, pack_n, inv_s, inv_n, side_s, side_n,
    face_x, face_y, gain_x, gain_y,
    halo_x, halo_y, red_x, red_y,
    send_sem, recv_sem, rx_send, rx_recv, ry_send, ry_recv, in_sem,
):
    nx, ny, nz = right_ref.shape
    gx = lax.axis_index("gx")
    gy = lax.axis_index("gy")
    has = (gx > 0, gx < ngx - 1, gy > 0, gy < ngy - 1)

    parts = next(p for p in (4, 2, 1) if nx % p == 0)
    span = nx // parts
    fetch_table = pltpu.make_async_copy(table_in, table_ref, in_sem.at[parts + 1])
    fetch_table.start()
    fetches = []
    for p in range(parts):
        rows = pl.ds(p * span, span)
        fetches.append(pltpu.make_async_copy(phase_in.at[rows], phase_ref.at[rows], in_sem.at[p]))
        fetches[p].start()
    fetch_right = pltpu.make_async_copy(right_in, right_ref, in_sem.at[parts])
    fetch_right.start()

    barrier = pltpu.get_barrier_semaphore()
    for k in range(1, ngx):
        pl.semaphore_signal(barrier, inc=1, device_id={"gx": lax.rem(gx + k, ngx)}, device_id_type=MESH)
    for k in range(1, ngy):
        pl.semaphore_signal(barrier, inc=1, device_id={"gy": lax.rem(gy + k, ngy)}, device_id_type=MESH)

    halves = 2 if nx % 16 == 0 else 1
    half = nx // halves
    pieces = {side: (None,) if side < 2 else tuple(range(halves)) for side in range(4)}

    def piece_of(ref, piece):
        return ref if piece is None else ref.at[pl.ds(piece * half, half)]

    def slot(side, piece):
        return side if piece is None else 2 + 2 * (side - 2) + piece

    def halo(e, side):
        return halo_x.at[e, side] if side < 2 else halo_y.at[e, side - 2]

    def copy_of(e, side, piece, src):
        axis, position = ("gx", gx) if side < 2 else ("gy", gy)
        step = -1 if side % 2 == 0 else 1
        return pltpu.make_async_remote_copy(
            src_ref=piece_of(src, piece),
            dst_ref=piece_of(halo(e, side ^ 1), piece),
            send_sem=send_sem.at[e, slot(side, piece)],
            recv_sem=recv_sem.at[e, slot(side ^ 1, piece)],
            device_id={axis: position + step},
            device_id_type=MESH,
        )

    sent = []

    def send(e, side, source, chosen=None):
        for piece in pieces[side] if chosen is None else (chosen,):
            copy = copy_of(e, side, piece, source)
            pl.when(has[side])(functools.partial(lambda c: c.start(), copy))
            sent.append((side, copy))

    def arrive(e, sides, chosen=None):
        for side in sides:
            for piece in pieces[side] if chosen is None else (chosen,):
                here = piece_of(halo(e, side), piece)
                dummy = pltpu.make_async_remote_copy(
                    src_ref=here,
                    dst_ref=here,
                    send_sem=send_sem.at[e, slot(side, piece)],
                    recv_sem=recv_sem.at[e, slot(side, piece)],
                    device_id={"gx": gx, "gy": gy},
                    device_id_type=MESH,
                )
                pl.when(has[side])(functools.partial(lambda c: c.wait_recv(), dummy))

    fetch_table.wait()

    t1, t2, t3 = (jnp.full((1, 1), table_ref[k], jnp.float32) for k in (1, 2, 3))
    q0 = 1.0 / jnp.full((1, 1), table_ref[0], jnp.float32)
    q1, q2, q3 = 1.0 / t1, 1.0 / t2, 1.0 / t3

    for side in range(4):
        def outside(side=side):
            for e in range(EXCHANGES):
                target = halo(e, side)
                fill = jnp.zeros(target.shape, jnp.float32)
                target[...] = fill + q0 if e == 0 else fill

        pl.when(jnp.logical_not(has[side]))(outside)

    def lookup_plane(i, _):
        labels = phase_ref[i]
        value = jnp.where(labels == 1, q1, jnp.where(labels == 2, q2, jnp.where(labels == 3, q3, q0)))
        rho[i] = value
        pack_s[0, pl.ds(i, 1), :] = value[0:1]
        pack_n[0, pl.ds(i, 1), :] = value[ny - 1 : ny]

    for p in range(parts):
        fetches[p].wait()
        loop(p * span, (p + 1) * span, lookup_plane)
    pl.semaphore_wait(barrier, ngx - 1 + ngy - 1)
    send(0, 2, pack_s.at[0])
    send(0, 3, pack_n.at[0])
    send(0, 0, rho.at[0])
    send(0, 1, rho.at[nx - 1])

    row = lax.broadcasted_iota(jnp.int32, (ny, nz), 0)
    lane = lax.broadcasted_iota(jnp.int32, (ny, nz), 1)
    zero = jnp.zeros((ny, nz), jnp.float32)
    cx[0] = zero
    cx[nx] = zero
    for c in range(3):
        for buffer in (ys, firsts, seconds):
            buffer[c, 0] = zero
            buffer[c, nx + 1] = zero

    def couple_x(i, _):
        cx[i] = 2.0 / (rho[i - 1] + rho[i])

    loop(1, nx, couple_x)
    fetch_right.wait()

    def right_rows(i, _):
        right = right_ref[i]
        side_s[4, pl.ds(i, 1), :] = right[0:1]
        side_n[4, pl.ds(i, 1), :] = right[ny - 1 : ny]

    loop(0, nx, right_rows)

    def couple_rest(i, _):
        here = rho[i]
        south = jnp.where(row == 0, 0.0, 2.0 / (here + pltpu.roll(here, 1, 0)))
        beside = jnp.where(lane == 0, q0, pltpu.roll(here, 1, 1))
        down = 2.0 / (here + beside)
        last = 2.0 / (here[:, nz - 128 :] + q0)
        last = jnp.concatenate([jnp.zeros((ny, nz - 128), jnp.float32), last], axis=1)
        inner = jnp.where(lane == 0, 0.0, down)
        cs[i] = south
        cd[i] = inner
        up = jnp.where(lane == nz - 1, last, pltpu.roll(inner, nz - 1, 1))
        d = cx[i] + cx[i + 1] + south + pltpu.roll(south, ny - 1, 0) + down + up
        diag[i] = d
        side_s[3, pl.ds(i, 1), :] = d[0:1]
        side_n[3, pl.ds(i, 1), :] = d[ny - 1 : ny]

    loop(0, nx, couple_rest)

    def scatter(ref, first, row_s, row_n):
        def one(i, _):
            ref[first + i, 0:1, :] = row_s[pl.ds(i, 1), :]
            ref[first + i, ny - 1 : ny, :] = row_n[pl.ds(i, 1), :]

        loop(1, nx - 1, one)

    def settle(e, ref, first, row_s, row_n, add_x, add_y, e_out=None):
        edge = (first, first + nx - 1)
        arrive(e, (0, 1))
        for side, i in ((0, 0), (1, nx - 1)):
            plane = ref[edge[side]] + add_x(side)
            ref[edge[side]] = plane
            row_s[i : i + 1, :] = plane[0:1]
            row_n[i : i + 1, :] = plane[ny - 1 : ny]
        for k, rows in ((0, row_s), (1, row_n)):
            for piece in pieces[2 + k]:
                arrive(e, (2 + k,), piece)
                part = slice(piece * half, (piece + 1) * half)
                rows[part] = rows[part] + add_y(k, part)
                if e_out is not None:
                    send(e_out, 2 + k, rows, piece)
        for side, i in ((0, 0), (1, nx - 1)):
            ref[edge[side], 0:1, :] = row_s[i : i + 1, :]
            ref[edge[side], ny - 1 : ny, :] = row_n[i : i + 1, :]
            if e_out is not None:
                send(e_out, side, ref.at[edge[side]])

    arrive(0, range(4))
    for side, plane in ((0, 0), (1, nx - 1)):
        face_x[side] = 2.0 / (rho[plane] + halo_x[0, side])
    face_y[0] = 2.0 / (pack_s[0] + halo_y[0, 0])
    face_y[1] = 2.0 / (pack_n[0] + halo_y[0, 1])
    ds_, dn_ = side_s.at[3], side_n.at[3]
    for side, plane in ((0, 0), (1, nx - 1)):
        whole = diag[plane] + face_x[side]
        diag[plane] = whole
        ds_[plane : plane + 1, :] = whole[0:1]
        dn_[plane : plane + 1, :] = whole[ny - 1 : ny]
    ds_[...] = ds_[...] + face_y[0]
    dn_[...] = dn_[...] + face_y[1]
    for plane in (0, nx - 1):
        diag[plane, 0:1, :] = ds_[plane : plane + 1, :]
        diag[plane, ny - 1 : ny, :] = dn_[plane : plane + 1, :]
    inv_s[...] = 1.0 / ds_[...]
    inv_n[...] = 1.0 / dn_[...]
    for side, plane in ((0, 0), (1, nx - 1)):
        inv[plane] = 1.0 / diag[plane]
        gain_x[side] = face_x[side] * inv[plane]
    gain_y[0] = face_y[0] * inv_s[...]
    gain_y[1] = face_y[1] * inv_n[...]

    def near(f, i):
        here = f[i + 1]
        south = cs[i]
        down = cd[i]
        return (
            (cx[i] * f[i] + cx[i + 1] * f[i + 2])
            + (south * pltpu.roll(here, 1, 0) + pltpu.roll(south * here, ny - 1, 0))
            + (down * pltpu.roll(here, 1, 1) + pltpu.roll(down * here, nz - 1, 1))
        )

    def send_y(e, y, plane_value, value_s, value_n):
        pack_s[e] = value_s * inv_s[...]
        send(e, 2, pack_s.at[e])
        pack_n[e] = value_n * inv_n[...]
        send(e, 3, pack_n.at[e])
        for side, plane in ((0, 0), (1, nx - 1)):
            y[plane + 1] = plane_value(plane) * inv[plane]
            send(e, side, y.at[plane + 1])

    def gained(scale, e):
        return (
            lambda s: (scale * gain_x[s]) * halo_x[e, s],
            lambda s, part: (scale * gain_y[s, part]) * halo_y[e, s, part],
        )

    def composite(c, e, between, image, image_of=lambda i, value: value, scale=lambda: -1.0):
        y, first, second = ys.at[c], firsts.at[c], seconds.at[c]

        def step_first(i, _):
            value = own_first * y[i + 1] + near_first * (inv[i] * near(y, i))
            first[i + 1] = value
            pack_s[e + 1, pl.ds(i, 1), :] = value[0:1]
            pack_n[e + 1, pl.ds(i, 1), :] = value[ny - 1 : ny]

        loop(0, nx, step_first)
        row_s, row_n = pack_s.at[e + 1], pack_n.at[e + 1]
        settle(e, first, 1, row_s, row_n, *gained(near_first, e), e + 1)
        scatter(first, 1, row_s, row_n)
        between(0)

        def step_second(i, _):
            value = own_second * first[i + 1] + base_second * y[i + 1] + push_second * (inv[i] * near(first, i))
            second[i + 1] = value
            pack_s[e + 2, pl.ds(i, 1), :] = value[0:1]
            pack_n[e + 2, pl.ds(i, 1), :] = value[ny - 1 : ny]

        loop(0, nx, step_second)
        row_s2, row_n2 = pack_s.at[e + 2], pack_n.at[e + 2]
        settle(e + 1, second, 1, row_s2, row_n2, *gained(push_second, e + 1), e + 2)
        scatter(second, 1, row_s2, row_n2)
        between(1)

        def step_image(i, _):
            value = image_of(i, diag[i] * second[i + 1] - near(second, i))
            image[i] = value
            side_s[c, pl.ds(i, 1), :] = value[0:1]
            side_n[c, pl.ds(i, 1), :] = value[ny - 1 : ny]

        loop(0, nx, step_image)
        settle(
            e + 2, image, 0, side_s.at[c], side_n.at[c],
            lambda s: scale() * (face_x[s] * halo_x[e + 2, s]),
            lambda s, part: scale() * (face_y[s, part] * halo_y[e + 2, s, part]),
        )

    def reduce_start(buffer, axis, position, count, send_sems, recv_sems):
        for k in range(1, count):
            reduce_copy(buffer, axis, position, count, k, send_sems, recv_sems).start()

    def reduce_copy(buffer, axis, position, count, k, send_sems, recv_sems):
        return pltpu.make_async_remote_copy(
            src_ref=buffer.at[0],
            dst_ref=buffer.at[k],
            send_sem=send_sems.at[k],
            recv_sem=recv_sems.at[k],
            device_id={axis: lax.rem(position + k, count)},
            device_id_type=MESH,
        )

    def reduce_end(buffer, axis, position, count, send_sems, recv_sems):
        value = buffer[0]
        for k in range(1, count):
            reduce_copy(buffer, axis, position, count, k, send_sems, recv_sems).wait()
            value = value + buffer[k]
        return value

    def over_x(t):
        return red_x.at[t], "gx", gx, ngx, rx_send.at[t], rx_recv.at[t]

    def over_y(t):
        return red_y.at[t], "gy", gy, ngy, ry_send.at[t], ry_recv.at[t]

    def put_sums(t, sums):
        for k in range(2):
            red_x[t, 0, k : k + 1, :] = jnp.sum(sums[k], axis=0, keepdims=True)
        reduce_start(*over_x(t))

    def relay(t):
        red_y[t, 0] = reduce_end(*over_x(t))
        reduce_start(*over_y(t))

    def take_sums(t):
        both = reduce_end(*over_y(t))
        return total(both[0:1]), total(both[1:2])

    send_y(1, ys.at[0], lambda p: right_ref[p], side_s[4], side_n[4])
    scatter(diag, 0, ds_, dn_)

    def start_plane(i, _):
        value = 1.0 / diag[i]
        inv[i] = value
        ys[0, i + 1] = right_ref[i] * value

    loop(1, nx - 1, start_plane)
    composite(0, 1, lambda k: None, images.at[0])

    w0, u0 = images.at[0], seconds.at[0]
    send_y(4, ys.at[1], lambda p: w0[p], side_s[0], side_n[0])
    scatter(w0, 0, side_s.at[0], side_n.at[0])
    tile = jnp.zeros((8, 128), jnp.float32)

    def second_plane(i, sums):
        w = w0[i]
        u = u0[i + 1]
        ys[1, i + 1] = w * inv[i]
        return sums[0] + fold(right_ref[i] * u), sums[1] + fold(w * u)

    sums = (tile, tile)
    for plane in (0, nx - 1):
        u = u0[plane + 1]
        sums = (sums[0] + fold(right_ref[plane] * u), sums[1] + fold(w0[plane] * u))
    put_sums(0, loop(1, nx - 1, second_plane, sums))
    composite(1, 4, lambda k: relay(0) if k == 0 else None, images.at[1])
    g0, h0 = take_sums(0)
    a0 = g0 / h0

    m0, n0 = seconds.at[1], images.at[1]
    for plane in (0, nx - 1):
        w_next[plane] = w0[plane] - a0 * n0[plane]
    send_y(7, ys.at[2], lambda p: w_next[p], side_s[0] - a0 * side_s[1], side_n[0] - a0 * side_n[1])
    scatter(n0, 0, side_s.at[1], side_n.at[1])

    def advance(i, sums):
        w = w_next[i]
        r = right_ref[i] - a0 * w0[i]
        u = u0[i + 1] - a0 * m0[i + 1]
        return sums[0] + fold(r * u), sums[1] + fold(w * u)

    def third_plane(i, sums):
        w = w0[i] - a0 * n0[i]
        w_next[i] = w
        ys[2, i + 1] = w * inv[i]
        return advance(i, sums)

    sums = (tile, tile)
    for plane in (0, nx - 1):
        sums = advance(plane, sums)
    put_sums(1, loop(1, nx - 1, third_plane, sums))
    found = []

    def last_between(k):
        if k == 0:
            relay(1)
            return
        g1, h1 = take_sums(1)
        b = g1 / g0
        a1 = g1 / (h1 - b * g1 / a0)
        found.extend((a1, b))

        def finish(i, _):
            u, m = u0[i + 1], m0[i + 1]
            u_next = u - a0 * m
            x_out[i] = a0 * u + a1 * (u_next + b * u)
            u_out[i] = u_next - a1 * (seconds[2, i + 1] + b * m)
            w = w0[i]
            r_out[i] = (right_ref[i] - a0 * w) - a1 * (w_next[i] + b * w)

        loop(0, nx, finish)

    composite(
        2, 7, last_between, w_out,
        lambda i, value: w_next[i] - found[0] * (value + found[1] * n0[i]),
        lambda: found[0],
    )
    scatter(w_out, 0, side_s.at[2], side_n.at[2])

    for side, copy in sent:
        pl.when(has[side])(functools.partial(lambda c: c.wait_send(), copy))


def deliver(parts, *refs):
    held, outs, sems = refs[:4], refs[4:8], refs[8]
    span = held[0].shape[0] // parts
    copies = []
    for k in range(4):
        for p in range(parts):
            rows = pl.ds(p * span, span)
            copies.append(pltpu.make_async_copy(held[k].at[rows], outs[k].at[rows], sems.at[k, p]))
            copies[-1].start()
    for copy in copies:
        copy.wait()


def solution(mesh):
    ngx, ngy = mesh.shape["gx"], mesh.shape["gy"]

    def local(right_side, phase, table):
        nx, ny, nz = right_side.shape
        f32 = jnp.float32
        block = pltpu.VMEM((nx, ny, nz), f32)
        three = pltpu.VMEM((3, nx + 2, ny, nz), f32)
        packed = pltpu.VMEM((EXCHANGES, nx, nz), f32)
        packed_one = pltpu.VMEM((nx, nz), f32)
        sides = pltpu.VMEM((5, nx, nz), f32)
        whole = pl.BlockSpec(memory_space=pltpu.VMEM)
        far = pl.BlockSpec(memory_space=pltpu.HBM)
        held = pl.pallas_call(
            functools.partial(kernel, ngx, ngy),
            out_shape=[block] * 4,
            in_specs=[far] * 3,
            out_specs=[whole] * 4,
            scratch_shapes=[
                block, pltpu.VMEM((nx, ny, nz), jnp.int32), pltpu.SMEM(table.shape, f32),
                three, pltpu.VMEM((2, nx, ny, nz), f32),
                block, pltpu.VMEM((nx + 1, ny, nz), f32), block, block, block, block,
                three, three, block,
                packed, packed, packed_one, packed_one, sides, sides,
                pltpu.VMEM((2, ny, nz), f32), pltpu.VMEM((2, nx, nz), f32),
                pltpu.VMEM((2, ny, nz), f32), pltpu.VMEM((2, nx, nz), f32),
                pltpu.VMEM((EXCHANGES, 2, ny, nz), f32), pltpu.VMEM((EXCHANGES, 2, nx, nz), f32),
                pltpu.VMEM((2, ngx, 2, 128), f32), pltpu.VMEM((2, ngy, 2, 128), f32),
                pltpu.SemaphoreType.DMA((EXCHANGES, 6)), pltpu.SemaphoreType.DMA((EXCHANGES, 6)),
                pltpu.SemaphoreType.DMA((2, ngx)), pltpu.SemaphoreType.DMA((2, ngx)),
                pltpu.SemaphoreType.DMA((2, ngy)), pltpu.SemaphoreType.DMA((2, ngy)),
                pltpu.SemaphoreType.DMA((6,)),
            ],
            compiler_params=pltpu.CompilerParams(
                collective_id=0, has_side_effects=True, vmem_limit_bytes=59 * 1024 * 1024 + 512 * 1024
            ),
        )(right_side, phase, table)
        parts = next(p for p in (2, 1) if nx % p == 0)
        return pl.pallas_call(
            functools.partial(deliver, parts),
            out_shape=[jax.ShapeDtypeStruct((nx, ny, nz), f32)] * 4,
            in_specs=[whole] * 4,
            out_specs=[far] * 4,
            scratch_shapes=[pltpu.SemaphoreType.DMA((4, parts))],
            compiler_params=pltpu.CompilerParams(vmem_limit_bytes=16 * 1024 * 1024),
        )(*held)

    spec = P("gx", "gy", None)
    return jax.shard_map(
        local, mesh=mesh, in_specs=(spec, spec, P()), out_specs=(spec,) * 4, check_vma=False
    )
```

```python
import functools

import jax
import jax.numpy as jnp
from jax import lax
from jax.experimental import pallas as pl
from jax.experimental.pallas import tpu as pltpu
from jax.sharding import PartitionSpec as P

MESH = pl.DeviceIdType.MESH

centre_value = 1.1
half_width = 0.9
ratio_sigma = centre_value / half_width
rho_first = 1.0 / ratio_sigma
rho_second = 1.0 / (2.0 * ratio_sigma - rho_first)
rho_third = 1.0 / (2.0 * ratio_sigma - rho_second)
start_scale = 1.0 / centre_value
keep_first = rho_second * rho_first
push_first = 2.0 * rho_second / half_width
keep_second = rho_third * rho_second
push_second = 2.0 * rho_third / half_width

own_first = start_scale * (1.0 + keep_first) + push_first * (1.0 - start_scale)
near_first = push_first * start_scale
own_second = 1.0 + keep_second - push_second
base_second = push_second - keep_second * start_scale

EXCHANGES = 10


def loop(low, high, body, carry=None):
    count = high - low
    unroll = next(u for u in (8, 6, 5, 4, 3, 2, 1) if count % u == 0)

    def step(k, value):
        for j in range(unroll):
            value = body(low + k * unroll + j, value)
        return value

    return lax.fori_loop(0, count // unroll, step, carry)


def fold(block):
    rows, lanes = block.shape
    tile = block[0:8]
    for k in range(1, rows // 8):
        tile = tile + block[8 * k : 8 * k + 8]
    out = tile[:, 0:128]
    for k in range(1, lanes // 128):
        out = out + tile[:, 128 * k : 128 * k + 128]
    return out


def total(row):
    return jnp.sum(row, axis=1, keepdims=True)


def kernel(
    ngx, ngy,
    right_in, phase_in, table_in,
    x_out, r_out, u_out, w_out,
    right_ref, phase_ref, table_ref,
    seconds, images,
    rho, cx, cs, cd, diag, inv,
    ys, firsts, w_next,
    pack_s, pack_n, inv_s, inv_n, side_s, side_n,
    face_x, face_y, gain_x, gain_y,
    halo_x, halo_y, red_x, red_y,
    send_sem, recv_sem, rx_send, rx_recv, ry_send, ry_recv, in_sem,
):
    nx, ny, nz = right_ref.shape
    gx = lax.axis_index("gx")
    gy = lax.axis_index("gy")
    has = (gx > 0, gx < ngx - 1, gy > 0, gy < ngy - 1)

    parts = next(p for p in (4, 2, 1) if nx % p == 0)
    span = nx // parts
    fetch_table = pltpu.make_async_copy(table_in, table_ref, in_sem.at[parts + 1])
    fetch_table.start()
    fetches = []
    for p in range(parts):
        rows = pl.ds(p * span, span)
        fetches.append(pltpu.make_async_copy(phase_in.at[rows], phase_ref.at[rows], in_sem.at[p]))
        fetches[p].start()
    fetch_right = pltpu.make_async_copy(right_in, right_ref, in_sem.at[parts])
    fetch_right.start()

    barrier = pltpu.get_barrier_semaphore()
    for k in range(1, ngx):
        pl.semaphore_signal(barrier, inc=1, device_id={"gx": lax.rem(gx + k, ngx)}, device_id_type=MESH)
    for k in range(1, ngy):
        pl.semaphore_signal(barrier, inc=1, device_id={"gy": lax.rem(gy + k, ngy)}, device_id_type=MESH)

    halves = 2 if nx % 16 == 0 else 1
    half = nx // halves
    pieces = {side: (None,) if side < 2 else tuple(range(halves)) for side in range(4)}

    def piece_of(ref, piece):
        return ref if piece is None else ref.at[pl.ds(piece * half, half)]

    def slot(side, piece):
        return side if piece is None else 2 + 2 * (side - 2) + piece

    def halo(e, side):
        return halo_x.at[e, side] if side < 2 else halo_y.at[e, side - 2]

    def copy_of(e, side, piece, src):
        axis, position = ("gx", gx) if side < 2 else ("gy", gy)
        step = -1 if side % 2 == 0 else 1
        return pltpu.make_async_remote_copy(
            src_ref=piece_of(src, piece),
            dst_ref=piece_of(halo(e, side ^ 1), piece),
            send_sem=send_sem.at[e, slot(side, piece)],
            recv_sem=recv_sem.at[e, slot(side ^ 1, piece)],
            device_id={axis: position + step},
            device_id_type=MESH,
        )

    sent = []

    def send(e, side, source, chosen=None):
        for piece in pieces[side] if chosen is None else (chosen,):
            copy = copy_of(e, side, piece, source)
            pl.when(has[side])(functools.partial(lambda c: c.start(), copy))
            sent.append((side, copy))

    def arrive(e, sides, chosen=None):
        for side in sides:
            for piece in pieces[side] if chosen is None else (chosen,):
                here = piece_of(halo(e, side), piece)
                dummy = pltpu.make_async_remote_copy(
                    src_ref=here,
                    dst_ref=here,
                    send_sem=send_sem.at[e, slot(side, piece)],
                    recv_sem=recv_sem.at[e, slot(side, piece)],
                    device_id={"gx": gx, "gy": gy},
                    device_id_type=MESH,
                )
                pl.when(has[side])(functools.partial(lambda c: c.wait_recv(), dummy))

    fetch_table.wait()

    t1, t2, t3 = (jnp.full((1, 1), table_ref[k], jnp.float32) for k in (1, 2, 3))
    q0 = 1.0 / jnp.full((1, 1), table_ref[0], jnp.float32)
    q1, q2, q3 = 1.0 / t1, 1.0 / t2, 1.0 / t3

    for side in range(4):
        def outside(side=side):
            for e in range(EXCHANGES):
                target = halo(e, side)
                fill = jnp.zeros(target.shape, jnp.float32)
                target[...] = fill + q0 if e == 0 else fill

        pl.when(jnp.logical_not(has[side]))(outside)

    def lookup_plane(i, _):
        labels = phase_ref[i]
        value = jnp.where(labels == 1, q1, jnp.where(labels == 2, q2, jnp.where(labels == 3, q3, q0)))
        rho[i] = value
        pack_s[0, pl.ds(i, 1), :] = value[0:1]
        pack_n[0, pl.ds(i, 1), :] = value[ny - 1 : ny]

    for p in range(parts):
        fetches[p].wait()
        loop(p * span, (p + 1) * span, lookup_plane)
    pl.semaphore_wait(barrier, ngx - 1 + ngy - 1)
    send(0, 2, pack_s.at[0])
    send(0, 3, pack_n.at[0])
    send(0, 0, rho.at[0])
    send(0, 1, rho.at[nx - 1])

    row = lax.broadcasted_iota(jnp.int32, (ny, nz), 0)
    lane = lax.broadcasted_iota(jnp.int32, (ny, nz), 1)
    zero = jnp.zeros((ny, nz), jnp.float32)
    cx[0] = zero
    cx[nx] = zero
    for c in range(3):
        for buffer in (ys, firsts, seconds):
            buffer[c, 0] = zero
            buffer[c, nx + 1] = zero

    def couple_x(i, _):
        cx[i] = 2.0 / (rho[i - 1] + rho[i])

    loop(1, nx, couple_x)
    fetch_right.wait()

    def right_rows(i, _):
        right = right_ref[i]
        side_s[4, pl.ds(i, 1), :] = right[0:1]
        side_n[4, pl.ds(i, 1), :] = right[ny - 1 : ny]

    loop(0, nx, right_rows)

    def couple_rest(i, _):
        here = rho[i]
        south = jnp.where(row == 0, 0.0, 2.0 / (here + pltpu.roll(here, 1, 0)))
        beside = jnp.where(lane == 0, q0, pltpu.roll(here, 1, 1))
        down = 2.0 / (here + beside)
        last = 2.0 / (here[:, nz - 128 :] + q0)
        last = jnp.concatenate([jnp.zeros((ny, nz - 128), jnp.float32), last], axis=1)
        inner = jnp.where(lane == 0, 0.0, down)
        cs[i] = south
        cd[i] = inner
        up = jnp.where(lane == nz - 1, last, pltpu.roll(inner, nz - 1, 1))
        d = cx[i] + cx[i + 1] + south + pltpu.roll(south, ny - 1, 0) + down + up
        diag[i] = d
        side_s[3, pl.ds(i, 1), :] = d[0:1]
        side_n[3, pl.ds(i, 1), :] = d[ny - 1 : ny]

    loop(0, nx, couple_rest)

    def scatter(ref, first, row_s, row_n):
        def one(i, _):
            ref[first + i, 0:1, :] = row_s[pl.ds(i, 1), :]
            ref[first + i, ny - 1 : ny, :] = row_n[pl.ds(i, 1), :]

        loop(1, nx - 1, one)

    def settle(e, ref, first, row_s, row_n, add_x, add_y, e_out=None):
        edge = (first, first + nx - 1)
        arrive(e, (0, 1))
        for side, i in ((0, 0), (1, nx - 1)):
            plane = ref[edge[side]] + add_x(side)
            ref[edge[side]] = plane
            row_s[i : i + 1, :] = plane[0:1]
            row_n[i : i + 1, :] = plane[ny - 1 : ny]
        for k, rows in ((0, row_s), (1, row_n)):
            for piece in pieces[2 + k]:
                arrive(e, (2 + k,), piece)
                part = slice(piece * half, (piece + 1) * half)
                rows[part] = rows[part] + add_y(k, part)
                if e_out is not None:
                    send(e_out, 2 + k, rows, piece)
        for side, i in ((0, 0), (1, nx - 1)):
            ref[edge[side], 0:1, :] = row_s[i : i + 1, :]
            ref[edge[side], ny - 1 : ny, :] = row_n[i : i + 1, :]
            if e_out is not None:
                send(e_out, side, ref.at[edge[side]])

    arrive(0, range(4))
    for side, plane in ((0, 0), (1, nx - 1)):
        face_x[side] = 2.0 / (rho[plane] + halo_x[0, side])
    face_y[0] = 2.0 / (pack_s[0] + halo_y[0, 0])
    face_y[1] = 2.0 / (pack_n[0] + halo_y[0, 1])
    ds_, dn_ = side_s.at[3], side_n.at[3]
    for side, plane in ((0, 0), (1, nx - 1)):
        whole = diag[plane] + face_x[side]
        diag[plane] = whole
        ds_[plane : plane + 1, :] = whole[0:1]
        dn_[plane : plane + 1, :] = whole[ny - 1 : ny]
    ds_[...] = ds_[...] + face_y[0]
    dn_[...] = dn_[...] + face_y[1]
    for plane in (0, nx - 1):
        diag[plane, 0:1, :] = ds_[plane : plane + 1, :]
        diag[plane, ny - 1 : ny, :] = dn_[plane : plane + 1, :]
    inv_s[...] = 1.0 / ds_[...]
    inv_n[...] = 1.0 / dn_[...]
    for side, plane in ((0, 0), (1, nx - 1)):
        inv[plane] = 1.0 / diag[plane]
        gain_x[side] = face_x[side] * inv[plane]
    gain_y[0] = face_y[0] * inv_s[...]
    gain_y[1] = face_y[1] * inv_n[...]

    def near(f, i):
        here = f[i + 1]
        south = cs[i]
        down = cd[i]
        return (
            (cx[i] * f[i] + cx[i + 1] * f[i + 2])
            + (south * pltpu.roll(here, 1, 0) + pltpu.roll(south * here, ny - 1, 0))
            + (down * pltpu.roll(here, 1, 1) + pltpu.roll(down * here, nz - 1, 1))
        )

    def send_y(e, y, plane_value, value_s, value_n):
        pack_s[e] = value_s * inv_s[...]
        send(e, 2, pack_s.at[e])
        pack_n[e] = value_n * inv_n[...]
        send(e, 3, pack_n.at[e])
        for side, plane in ((0, 0), (1, nx - 1)):
            y[plane + 1] = plane_value(plane) * inv[plane]
            send(e, side, y.at[plane + 1])

    def gained(scale, e):
        return (
            lambda s: (scale * gain_x[s]) * halo_x[e, s],
            lambda s, part: (scale * gain_y[s, part]) * halo_y[e, s, part],
        )

    def composite(c, e, between, image, image_of=lambda i, value: value, scale=lambda: -1.0):
        y, first, second = ys.at[c], firsts.at[c], seconds.at[c]

        def step_first(i, _):
            value = own_first * y[i + 1] + near_first * (inv[i] * near(y, i))
            first[i + 1] = value
            pack_s[e + 1, pl.ds(i, 1), :] = value[0:1]
            pack_n[e + 1, pl.ds(i, 1), :] = value[ny - 1 : ny]

        loop(0, nx, step_first)
        row_s, row_n = pack_s.at[e + 1], pack_n.at[e + 1]
        settle(e, first, 1, row_s, row_n, *gained(near_first, e), e + 1)
        scatter(first, 1, row_s, row_n)
        between(0)

        def step_second(i, _):
            value = own_second * first[i + 1] + base_second * y[i + 1] + push_second * (inv[i] * near(first, i))
            second[i + 1] = value
            pack_s[e + 2, pl.ds(i, 1), :] = value[0:1]
            pack_n[e + 2, pl.ds(i, 1), :] = value[ny - 1 : ny]

        loop(0, nx, step_second)
        row_s2, row_n2 = pack_s.at[e + 2], pack_n.at[e + 2]
        settle(e + 1, second, 1, row_s2, row_n2, *gained(push_second, e + 1), e + 2)
        scatter(second, 1, row_s2, row_n2)
        between(1)

        def step_image(i, _):
            value = image_of(i, diag[i] * second[i + 1] - near(second, i))
            image[i] = value
            side_s[c, pl.ds(i, 1), :] = value[0:1]
            side_n[c, pl.ds(i, 1), :] = value[ny - 1 : ny]

        loop(0, nx, step_image)
        settle(
            e + 2, image, 0, side_s.at[c], side_n.at[c],
            lambda s: scale() * (face_x[s] * halo_x[e + 2, s]),
            lambda s, part: scale() * (face_y[s, part] * halo_y[e + 2, s, part]),
        )

    def reduce_start(buffer, axis, position, count, send_sems, recv_sems):
        for k in range(1, count):
            reduce_copy(buffer, axis, position, count, k, send_sems, recv_sems).start()

    def reduce_copy(buffer, axis, position, count, k, send_sems, recv_sems):
        return pltpu.make_async_remote_copy(
            src_ref=buffer.at[0],
            dst_ref=buffer.at[k],
            send_sem=send_sems.at[k],
            recv_sem=recv_sems.at[k],
            device_id={axis: lax.rem(position + k, count)},
            device_id_type=MESH,
        )

    def reduce_end(buffer, axis, position, count, send_sems, recv_sems):
        value = buffer[0]
        for k in range(1, count):
            reduce_copy(buffer, axis, position, count, k, send_sems, recv_sems).wait()
            value = value + buffer[k]
        return value

    def over_x(t):
        return red_x.at[t], "gx", gx, ngx, rx_send.at[t], rx_recv.at[t]

    def over_y(t):
        return red_y.at[t], "gy", gy, ngy, ry_send.at[t], ry_recv.at[t]

    def put_sums(t, sums):
        for k in range(2):
            red_x[t, 0, k : k + 1, :] = jnp.sum(sums[k], axis=0, keepdims=True)
        reduce_start(*over_x(t))

    def relay(t):
        red_y[t, 0] = reduce_end(*over_x(t))
        reduce_start(*over_y(t))

    def take_sums(t):
        both = reduce_end(*over_y(t))
        return total(both[0:1]), total(both[1:2])

    send_y(1, ys.at[0], lambda p: right_ref[p], side_s[4], side_n[4])
    scatter(diag, 0, ds_, dn_)

    def start_plane(i, _):
        value = 1.0 / diag[i]
        inv[i] = value
        ys[0, i + 1] = right_ref[i] * value

    loop(1, nx - 1, start_plane)
    composite(0, 1, lambda k: None, images.at[0])

    w0, u0 = images.at[0], seconds.at[0]
    send_y(4, ys.at[1], lambda p: w0[p], side_s[0], side_n[0])
    scatter(w0, 0, side_s.at[0], side_n.at[0])
    tile = jnp.zeros((8, 128), jnp.float32)

    def second_plane(i, sums):
        w = w0[i]
        u = u0[i + 1]
        ys[1, i + 1] = w * inv[i]
        return sums[0] + fold(right_ref[i] * u), sums[1] + fold(w * u)

    sums = (tile, tile)
    for plane in (0, nx - 1):
        u = u0[plane + 1]
        sums = (sums[0] + fold(right_ref[plane] * u), sums[1] + fold(w0[plane] * u))
    put_sums(0, loop(1, nx - 1, second_plane, sums))
    composite(1, 4, lambda k: relay(0) if k == 0 else None, images.at[1])
    g0, h0 = take_sums(0)
    a0 = g0 / h0

    m0, n0 = seconds.at[1], images.at[1]
    for plane in (0, nx - 1):
        w_next[plane] = w0[plane] - a0 * n0[plane]
    send_y(7, ys.at[2], lambda p: w_next[p], side_s[0] - a0 * side_s[1], side_n[0] - a0 * side_n[1])
    scatter(n0, 0, side_s.at[1], side_n.at[1])

    def advance(i, sums):
        w = w_next[i]
        r = right_ref[i] - a0 * w0[i]
        u = u0[i + 1] - a0 * m0[i + 1]
        return sums[0] + fold(r * u), sums[1] + fold(w * u)

    def third_plane(i, sums):
        w = w0[i] - a0 * n0[i]
        w_next[i] = w
        ys[2, i + 1] = w * inv[i]
        return advance(i, sums)

    sums = (tile, tile)
    for plane in (0, nx - 1):
        sums = advance(plane, sums)
    put_sums(1, loop(1, nx - 1, third_plane, sums))
    found = []

    def last_between(k):
        if k == 0:
            relay(1)
            return
        g1, h1 = take_sums(1)
        b = g1 / g0
        a1 = g1 / (h1 - b * g1 / a0)
        found.extend((a1, b))

        def finish(i, _):
            u, m = u0[i + 1], m0[i + 1]
            u_next = u - a0 * m
            x_out[i] = a0 * u + a1 * (u_next + b * u)
            u_out[i] = u_next - a1 * (seconds[2, i + 1] + b * m)
            w = w0[i]
            r_out[i] = (right_ref[i] - a0 * w) - a1 * (w_next[i] + b * w)

        loop(0, nx, finish)

    composite(
        2, 7, last_between, w_out,
        lambda i, value: w_next[i] - found[0] * (value + found[1] * n0[i]),
        lambda: found[0],
    )
    scatter(w_out, 0, side_s.at[2], side_n.at[2])

    for side, copy in sent:
        pl.when(has[side])(functools.partial(lambda c: c.wait_send(), copy))


def deliver(parts, *refs):
    held, outs, sems = refs[:4], refs[4:8], refs[8]
    span = held[0].shape[0] // parts
    copies = []
    for k in range(4):
        for p in range(parts):
            rows = pl.ds(p * span, span)
            copies.append(pltpu.make_async_copy(held[k].at[rows], outs[k].at[rows], sems.at[k, p]))
            copies[-1].start()
    for copy in copies:
        copy.wait()


def solution(mesh):
    ngx, ngy = mesh.shape["gx"], mesh.shape["gy"]

    def local(right_side, phase, table):
        nx, ny, nz = right_side.shape
        f32 = jnp.float32
        block = pltpu.VMEM((nx, ny, nz), f32)
        three = pltpu.VMEM((3, nx + 2, ny, nz), f32)
        packed = pltpu.VMEM((EXCHANGES, nx, nz), f32)
        packed_one = pltpu.VMEM((nx, nz), f32)
        sides = pltpu.VMEM((5, nx, nz), f32)
        whole = pl.BlockSpec(memory_space=pltpu.VMEM)
        far = pl.BlockSpec(memory_space=pltpu.HBM)
        held = pl.pallas_call(
            functools.partial(kernel, ngx, ngy),
            out_shape=[block] * 4,
            in_specs=[far] * 3,
            out_specs=[whole] * 4,
            scratch_shapes=[
                block, pltpu.VMEM((nx, ny, nz), jnp.int32), pltpu.SMEM(table.shape, f32),
                three, pltpu.VMEM((2, nx, ny, nz), f32),
                block, pltpu.VMEM((nx + 1, ny, nz), f32), block, block, block, block,
                three, three, block,
                packed, packed, packed_one, packed_one, sides, sides,
                pltpu.VMEM((2, ny, nz), f32), pltpu.VMEM((2, nx, nz), f32),
                pltpu.VMEM((2, ny, nz), f32), pltpu.VMEM((2, nx, nz), f32),
                pltpu.VMEM((EXCHANGES, 2, ny, nz), f32), pltpu.VMEM((EXCHANGES, 2, nx, nz), f32),
                pltpu.VMEM((2, ngx, 2, 128), f32), pltpu.VMEM((2, ngy, 2, 128), f32),
                pltpu.SemaphoreType.DMA((EXCHANGES, 6)), pltpu.SemaphoreType.DMA((EXCHANGES, 6)),
                pltpu.SemaphoreType.DMA((2, ngx)), pltpu.SemaphoreType.DMA((2, ngx)),
                pltpu.SemaphoreType.DMA((2, ngy)), pltpu.SemaphoreType.DMA((2, ngy)),
                pltpu.SemaphoreType.DMA((6,)),
            ],
            compiler_params=pltpu.CompilerParams(
                collective_id=0, has_side_effects=True, vmem_limit_bytes=59 * 1024 * 1024 + 512 * 1024
            ),
        )(right_side, phase, table)
        parts = next(p for p in (2, 1) if nx % p == 0)
        return pl.pallas_call(
            functools.partial(deliver, parts),
            out_shape=[jax.ShapeDtypeStruct((nx, ny, nz), f32)] * 4,
            in_specs=[whole] * 4,
            out_specs=[far] * 4,
            scratch_shapes=[pltpu.SemaphoreType.DMA((4, parts))],
            compiler_params=pltpu.CompilerParams(vmem_limit_bytes=16 * 1024 * 1024),
        )(*held)

    spec = P("gx", "gy", None)
    return jax.shard_map(
        local, mesh=mesh, in_specs=(spec, spec, P()), out_specs=(spec,) * 4, check_vma=False
    )
```
